512 devices in a mesh: blk: 256 (over y, x, z), tp: 2 (over core).
Axes of the slice: x: 4, y: 8, z: 8, core: 2. Of those that a mesh axis runs over, the one named last changes fastest.
Arguments:
- document_query: bfloat16 [131072, 2048], P('blk', 'tp'), may hold values from -16 to 16
- document_key: bfloat16 [131072, 512], P('blk', 'tp'), may hold values from -250 to 250
- document_value: bfloat16 [131072, 512], P('blk', 'tp'), may hold values from -6 to 6
- query_token_query: bfloat16 [4, 2048], P(None, 'tp'), may hold values from -6 to 6
- query_token_key: bfloat16 [4, 512], P(None, 'tp'), may hold values from -16 to 16
- query_token_value: bfloat16 [4, 512], P(None, 'tp'), may hold values from -6 to 6
Outputs:
- ctx_out: bfloat16 [131072, 2048], P('blk', 'tp')
- answer: bfloat16 [4, 2048], replicated
The draws below stay inside these ranges and needn't reach their ends.
All inputs are finite; a program needn't handle non-finite values.
Results may differ from the reference program's by a relative error of at most 0.0046.
Values may be sent and summed in bfloat16 or wider, within the bound.
No kernel may reach another device: no remote copies, remote signals or barrier semaphores. Data moves between devices by JAX's collectives and lax.ppermute only.
A program may use at most 64 MiB of HBM per device.

```python
import math
import jax
import jax.numpy as jnp
from jax import lax

HQ = 16
KEY_HEADS = 4
HEAD_SIZE = 128
QUERY_PER_KEY = 4
QUERY_TOKENS = 4
BLOCK_TOKENS = 512
DOCUMENT_TOKENS = 131072
N_BLK = 256


def needle_plan(key):
    base_key = jax.random.fold_in(key, 0)
    row_key = jax.random.fold_in(key, 1)
    order_key = jax.random.fold_in(key, 4)
    base_offset = jax.random.truncated_normal(base_key, -6.0, 6.0, (QUERY_TOKENS, HQ, HEAD_SIZE), jnp.float32)
    pairs = QUERY_TOKENS * HQ
    stride = max(DOCUMENT_TOKENS // pairs, 2)
    order = jax.random.permutation(order_key, pairs).astype(jnp.int32)
    starts = order * DOCUMENT_TOKENS // pairs
    offsets = jax.random.randint(row_key, (pairs,), 1, stride)
    rows = jnp.clip(starts + offsets, 1, DOCUMENT_TOKENS - 1).astype(jnp.int32).reshape(QUERY_TOKENS, HQ)
    return (base_offset, rows)


def draw_document_key(key, part):
    base_offset, rows = needle_plan(key)
    key = jax.random.fold_in(key, 11)
    random_noise = jax.random.truncated_normal(key, -6.0, 6.0, (DOCUMENT_TOKENS, KEY_HEADS, HEAD_SIZE), jnp.float32)
    strong = jnp.full((QUERY_TOKENS, HQ), math.log(DOCUMENT_TOKENS) + 2.5, jnp.float32)
    second = jnp.zeros((QUERY_TOKENS, HQ), jnp.float32)
    heads = jnp.broadcast_to(jnp.arange(HQ) // QUERY_PER_KEY, (QUERY_TOKENS, HQ))
    factor = float(HEAD_SIZE) ** (-0.5)
    random_noise = random_noise.at[rows, heads].add((strong * factor)[..., None] * base_offset)
    random_noise = random_noise.at[rows - 1, heads].add((second * factor)[..., None] * base_offset)
    return jnp.clip(random_noise, -250.0, 250.0).reshape(DOCUMENT_TOKENS, KEY_HEADS * HEAD_SIZE).astype(jnp.bfloat16)


def draw_document_query(key, part):
    key = jax.random.fold_in(key, 12)
    random_noise = jax.random.truncated_normal(key, -6.0, 6.0, (DOCUMENT_TOKENS, HQ, HEAD_SIZE), jnp.float32)
    return jnp.clip(random_noise, -16.0, 16.0).reshape(DOCUMENT_TOKENS, HQ * HEAD_SIZE).astype(jnp.bfloat16)


def draw_query_token_query(key, part):
    base_offset, rows = needle_plan(key)
    return base_offset.reshape(QUERY_TOKENS, HQ * HEAD_SIZE).astype(jnp.bfloat16)


def draw_query_token_key(key, part):
    base_offset, rows = needle_plan(key)
    key = jax.random.fold_in(key, 14)
    random_noise = jax.random.truncated_normal(key, -6.0, 6.0, (QUERY_TOKENS, KEY_HEADS, HEAD_SIZE), jnp.float32)
    query_average = jnp.mean(base_offset.reshape(QUERY_TOKENS, KEY_HEADS, QUERY_PER_KEY, HEAD_SIZE), axis=2)
    factor = QUERY_PER_KEY * math.log(DOCUMENT_TOKENS) / math.sqrt(HEAD_SIZE)
    final_output = random_noise + factor * query_average
    return jnp.clip(final_output, -16.0, 16.0).reshape(QUERY_TOKENS, KEY_HEADS * HEAD_SIZE).astype(jnp.bfloat16)


def block_scale(stream_key, shape, cuts, smallest, high):
    factor_of, own = 1.0, jax.random.fold_in(stream_key, 6)
    for axis_at, blocks in cuts:
        steps = jnp.exp(jax.random.uniform(jax.random.fold_in(own, axis_at), (blocks,), jnp.float32, smallest / len(cuts), high / len(cuts)))
        factor_of = factor_of * jnp.repeat(steps, shape[axis_at] // blocks).reshape([-1 if axis == axis_at else 1 for axis in range(len(shape))])
    return factor_of


def bell_draw(rng, shape, spread, reach, shards=(), kind=jnp.bfloat16):
    result = jax.random.normal(rng, shape, jnp.float32) * spread
    if len(shards) > 0:
        result = block_scale(rng, shape, shards, -0.22, 0.18) * result
    return jnp.clip(result, min=-reach, max=reach).astype(kind)


def setup_inputs(seed: int = 0) -> dict:
    key_of = jax.random.split(jax.random.key(seed), 7)
    document_query = draw_document_query(jax.random.fold_in(key_of[6], 71), 0)
    document_key = draw_document_key(jax.random.fold_in(key_of[6], 71), 0)
    document_value = bell_draw(key_of[2], (DOCUMENT_TOKENS, KEY_HEADS * HEAD_SIZE), 1.0, 6.0, ((0, 256), (1, 2)))
    query_token_query = draw_query_token_query(jax.random.fold_in(key_of[6], 71), 0)
    query_token_key = draw_query_token_key(jax.random.fold_in(key_of[6], 71), 0)
    query_token_value = bell_draw(key_of[5], (QUERY_TOKENS, KEY_HEADS * HEAD_SIZE), 1.0, 6.0, ((1, 2),))
    return {"document_query": document_query, "document_key": document_key, "document_value": document_value, "query_token_query": query_token_query, "query_token_key": query_token_key, "query_token_value": query_token_value}


def head_attend(q_head, k_head, v_head, allowed):
    scale = float(q_head.shape[-1]) ** -0.5
    scores = jnp.einsum("tgd,sd->gts", q_head.astype(jnp.float32), k_head.astype(jnp.float32)) * scale
    scores = jnp.where(allowed[None], scores, -jnp.inf)
    peak = jnp.max(scores, axis=-1, keepdims=True)
    expo = jnp.exp(scores - peak)
    total = jnp.sum(expo, axis=-1)
    probs = expo.astype(jnp.bfloat16)
    mixed = jnp.einsum("gts,sd->gtd", probs.astype(jnp.float32), v_head.astype(jnp.float32))
    return peak[..., 0], total, mixed


def partial_results(query_rows, key_rows, value_rows, allowed):
    peaks, totals, mixes = [], [], []
    for group_heads in range(key_rows.shape[1]):
        peak, total, mixed = head_attend(query_rows[:, group_heads], key_rows[:, group_heads], value_rows[:, group_heads], allowed)
        peaks.append(peak)
        totals.append(total)
        mixes.append(mixed)
    return jnp.stack(peaks), jnp.stack(totals), jnp.stack(mixes)


def reference(document_query, document_key, document_value, query_token_query, query_token_key, query_token_value):
    block_list = N_BLK
    query_rows = document_query.reshape(block_list, BLOCK_TOKENS, KEY_HEADS, QUERY_PER_KEY, HEAD_SIZE)
    key_rows = document_key.reshape(block_list, BLOCK_TOKENS, KEY_HEADS, HEAD_SIZE)
    value_rows = document_value.reshape(block_list, BLOCK_TOKENS, KEY_HEADS, HEAD_SIZE)
    anchor_key = key_rows[0]
    anchor_value = value_rows[0]
    line = jnp.arange(BLOCK_TOKENS)[:, None]
    column = jnp.arange(2 * BLOCK_TOKENS)[None, :]

    def one_block(item):
        block_q, block_k, block_v, index = item
        all_keys = jnp.concatenate([anchor_key, block_k], 0)
        all_values = jnp.concatenate([anchor_value, block_v], 0)
        allowed = jnp.where(column < BLOCK_TOKENS, index > 0, column - BLOCK_TOKENS <= line)
        outs = []
        for group_heads in range(KEY_HEADS):
            peak, total, mixed = head_attend(block_q[:, group_heads], all_keys[:, group_heads], all_values[:, group_heads], allowed)
            outs.append(jnp.transpose(mixed / total[..., None], (1, 0, 2)))
        return jnp.stack(outs, 1).reshape(BLOCK_TOKENS, HQ * HEAD_SIZE).astype(jnp.bfloat16)

    ctx_out = lax.map(one_block, (query_rows, key_rows, value_rows, jnp.arange(block_list, dtype=jnp.int32)))
    ctx_out = ctx_out.reshape(DOCUMENT_TOKENS, HQ * HEAD_SIZE)

    fresh_tokens = query_token_query.reshape(QUERY_TOKENS, KEY_HEADS, QUERY_PER_KEY, HEAD_SIZE)
    full = jnp.ones((QUERY_TOKENS, BLOCK_TOKENS), dtype=bool)

    def block_part(item):
        block_k, block_v = item
        return partial_results(fresh_tokens, block_k, block_v, full)

    peak_all, total_all, mixed_all = lax.map(block_part, (key_rows, value_rows))
    top = jnp.max(peak_all, axis=0)
    weight = jnp.exp(peak_all - top)
    total = jnp.sum(total_all * weight, axis=0)
    merged = jnp.sum(mixed_all * weight[..., None], axis=0)
    causal_mask = jnp.arange(QUERY_TOKENS)[:, None] >= jnp.arange(QUERY_TOKENS)[None, :]
    own_block_maximum, own_block_sum, own_block_output = partial_results(fresh_tokens, query_token_key.reshape(QUERY_TOKENS, KEY_HEADS, HEAD_SIZE), query_token_value.reshape(QUERY_TOKENS, KEY_HEADS, HEAD_SIZE), causal_mask)
    final_top = jnp.maximum(top, own_block_maximum)
    first = jnp.exp(top - final_top)
    second = jnp.exp(own_block_maximum - final_top)
    total = total * first + own_block_sum * second
    merged = merged * first[..., None] + own_block_output * second[..., None]
    answer = jnp.transpose(merged / total[..., None], (2, 0, 1, 3)).reshape(QUERY_TOKENS, HQ * HEAD_SIZE).astype(jnp.bfloat16)
    return ctx_out, answer
```

```python
import math

import jax
import jax.numpy as jnp
from jax import lax
from jax.experimental import pallas as pl
from jax.experimental.pallas import tpu as pltpu
from jax.sharding import Mesh, PartitionSpec as P

HEAD_SIZE = 128
QUERY_PER_KEY = 4
QUERY_TOKENS = 4
SIZES = (8, 4, 8)
NEG = -1e30
F32 = jnp.float32
BF16 = jnp.bfloat16
SCALE = HEAD_SIZE**-0.5
LOG2E = math.log2(math.e)
VMEM_LIMIT = 40 * 1024 * 1024


def dot_nt(a, b):
    return lax.dot_general(a, b, (((1,), (1,)), ((), ())), preferred_element_type=F32)


def block_index():
    return (lax.axis_index("y") * SIZES[1] + lax.axis_index("x")) * SIZES[2] + lax.axis_index("z")


def parts_of(value, count):
    terms = []
    for _ in range(count - 1):
        term = value.astype(BF16).astype(F32)
        terms.append(term)
        value = value - term
    return terms + [value]


def record_rows(peak, total, mixed):
    return parts_of(mixed, 2) + parts_of(peak, 3) + parts_of(total, 2)


def merge_records(ref, count, stride):
    row = lambda k: ref[pl.ds(k, count, stride=stride), :]
    mixed = row(0) + row(1)
    peak = (row(2) + row(3)) + row(4)
    total = row(5) + row(6)
    top = jnp.max(peak, axis=0, keepdims=True)
    weight = jnp.exp(peak - top)
    return (
        top,
        jnp.sum(total * weight, axis=0, keepdims=True),
        jnp.sum(mixed * weight, axis=0, keepdims=True),
    )


def local_kernel(qt_ref, qk_ref, qv_ref, k_ref, v_ref, out_ref, rec_ref, q_ref):
    heads = qt_ref.shape[1] // HEAD_SIZE
    rows = k_ref.shape[0]
    chunk = rows // (heads * QUERY_TOKENS)
    out_ref[:, : k_ref.shape[1]] = k_ref[...]
    out_ref[:, k_ref.shape[1] : 2 * k_ref.shape[1]] = v_ref[...]
    for h in range(heads):
        q_ref[h * QUERY_TOKENS : (h + 1) * QUERY_TOKENS, :] = qt_ref[
            :, h * HEAD_SIZE : (h + 1) * HEAD_SIZE
        ].astype(F32)
    rec_ref[...] = jnp.zeros_like(rec_ref)
    first_block = block_index() == 0
    group = QUERY_PER_KEY * QUERY_TOKENS
    token = lax.broadcasted_iota(jnp.int32, (group, 1), 0) % QUERY_TOKENS
    for kv in range(heads // QUERY_PER_KEY):
        cols = slice(kv * HEAD_SIZE, (kv + 1) * HEAD_SIZE)
        q = q_ref[kv * group : (kv + 1) * group, :]
        scores = dot_nt(q.astype(BF16), k_ref[:, cols]) * SCALE
        peak = jnp.max(scores, axis=-1, keepdims=True)
        new_k = qk_ref[:, cols].astype(F32)
        new_v = qv_ref[:, cols].astype(F32)
        own = []
        for j in range(QUERY_TOKENS):
            s = jnp.sum(q * new_k[j : j + 1, :], axis=-1, keepdims=True) * SCALE
            own.append(jnp.where(jnp.logical_and(token >= j, first_block), s, NEG))
        top = peak
        for s in own:
            top = jnp.maximum(top, s)
        expo = jnp.exp(scores - top)
        total = jnp.sum(expo, axis=-1, keepdims=True)
        mixed = jnp.dot(expo.astype(BF16), v_ref[:, cols], preferred_element_type=F32)
        for j, s in enumerate(own):
            e = jnp.exp(s - top)
            total = total + e
            mixed = mixed + e.astype(BF16).astype(F32) * new_v[j : j + 1, :]
        full = (group, HEAD_SIZE)
        for k, value in enumerate(
            record_rows(jnp.broadcast_to(top, full), jnp.broadcast_to(total, full), mixed)
        ):
            rec_ref[pl.ds(kv * group * chunk + k, group, stride=chunk), :] = value
    out_ref[:, 2 * k_ref.shape[1] :] = rec_ref[...].astype(BF16)


def middle_kernel(peers, copies, last, rec_in_ref, chunk_ref, out_ref, in_ref, rec_ref):
    chunk, width = chunk_ref.shape
    in_ref[...] = rec_in_ref[...].astype(F32)
    peak, total, mixed = merge_records(in_ref, peers, chunk)
    if last:
        rec_ref[...] = jnp.broadcast_to(mixed / total, rec_ref.shape)
    else:
        rec_ref[...] = jnp.zeros_like(rec_ref)
        for k, value in enumerate(record_rows(peak, total, mixed)):
            rec_ref[k : k + 1, :] = value
    record = rec_ref[...].astype(BF16)
    piece = chunk_ref[...]
    for i in range(copies):
        out_ref[i * chunk : (i + 1) * chunk, :width] = piece
        out_ref[i * chunk : (i + 1) * chunk, width:] = record


def middle(received, chunk, width, peers, copies, last):
    def kernel(*refs):
        middle_kernel(peers, copies, last, *refs)

    total = received.shape[1]
    return pl.pallas_call(
        kernel,
        grid=(1,),
        out_shape=jax.ShapeDtypeStruct((copies * chunk, total), BF16),
        in_specs=[
            pl.BlockSpec((peers * chunk, HEAD_SIZE), lambda i: (0, width // HEAD_SIZE)),
            pl.BlockSpec((chunk, width), lambda i: (0, 0)),
        ],
        out_specs=pl.BlockSpec((copies * chunk, total), lambda i: (0, 0)),
        scratch_shapes=[
            pltpu.VMEM((peers * chunk, HEAD_SIZE), F32),
            pltpu.VMEM((chunk, HEAD_SIZE), F32),
        ],
        compiler_params=pltpu.CompilerParams(vmem_limit_bytes=VMEM_LIMIT),
        name="merge_last" if last else "merge_first",
    )(received, received)


def answer_kernel(rec_in_ref, out_ref, in_ref):
    heads = out_ref.shape[1] // HEAD_SIZE
    count = heads * QUERY_TOKENS
    in_ref[...] = rec_in_ref[...].astype(F32)
    rows = in_ref[pl.ds(0, count, stride=in_ref.shape[0] // count), :]
    for h in range(heads):
        out_ref[:, h * HEAD_SIZE : (h + 1) * HEAD_SIZE] = rows[
            h * QUERY_TOKENS : (h + 1) * QUERY_TOKENS
        ].astype(BF16)


def attend_kernel(q_ref, k0_ref, v0_ref, k_ref, v_ref, out_ref):
    rows = q_ref.shape[0]
    step = 128
    off = jnp.where(block_index() > 0, 0.0, -NEG).astype(F32)
    factor = SCALE * LOG2E
    line = lax.broadcasted_iota(jnp.int32, (step, step), 0)
    column = lax.broadcasted_iota(jnp.int32, (step, step), 1)
    k0, v0 = k0_ref[...], v0_ref[...]
    for h in range(q_ref.shape[1] // HEAD_SIZE):
        cols = slice(h * HEAD_SIZE, (h + 1) * HEAD_SIZE)
        for i in range(rows // step):
            at = i * step
            q = q_ref[at : at + step, cols]
            far = dot_nt(q, k0)
            diag = jnp.where(column <= line, dot_nt(q, k_ref[at : at + step, :]), NEG)
            peak = jnp.max(diag, axis=-1, keepdims=True)
            if i:
                near = dot_nt(q, k_ref[:at, :])
                peak = jnp.maximum(peak, jnp.max(near, axis=-1, keepdims=True))
            peak = jnp.maximum(peak, jnp.max(far, axis=-1, keepdims=True) - off)
            base = peak * factor
            e = jnp.exp2(diag * factor - base)
            total = jnp.sum(e, axis=-1, keepdims=True)
            mixed = jnp.dot(
                e.astype(BF16), v_ref[at : at + step, :], preferred_element_type=F32
            )
            if i:
                e = jnp.exp2(near * factor - base)
                total += jnp.sum(e, axis=-1, keepdims=True)
                mixed += jnp.dot(e.astype(BF16), v_ref[:at, :], preferred_element_type=F32)
            e = jnp.exp2(far * factor - (base + off))
            total += jnp.sum(e, axis=-1, keepdims=True)
            mixed += jnp.dot(e.astype(BF16), v0, preferred_element_type=F32)
            out_ref[at : at + step, cols] = (mixed / total).astype(BF16)


def attend(document_query, received, document_key, document_value):
    rows, width = document_query.shape
    heads_kv = document_key.shape[1] // HEAD_SIZE
    per_step = 2
    steps = width // HEAD_SIZE // per_step
    share = steps // heads_kv
    wide = pl.BlockSpec((rows, per_step * HEAD_SIZE), lambda i: (0, i))
    narrow = lambda first: pl.BlockSpec((rows, HEAD_SIZE), lambda i: (0, first + i // share))
    return pl.pallas_call(
        attend_kernel,
        grid=(steps,),
        out_shape=jax.ShapeDtypeStruct((rows, width), BF16),
        in_specs=[wide, narrow(0), narrow(heads_kv), narrow(0), narrow(0)],
        out_specs=wide,
        compiler_params=pltpu.CompilerParams(vmem_limit_bytes=VMEM_LIMIT),
        name="attend",
    )(document_query, received, received, document_key, document_value)


def body(
    document_query,
    document_key,
    document_value,
    query_token_query,
    query_token_key,
    query_token_value,
):
    rows, width = document_key.shape
    plane = SIZES[1] * SIZES[2]
    chunk = rows // plane
    full = 2 * width + HEAD_SIZE
    send = pl.pallas_call(
        local_kernel,
        out_shape=jax.ShapeDtypeStruct((rows, full), BF16),
        scratch_shapes=[
            pltpu.VMEM((rows, HEAD_SIZE), F32),
            pltpu.VMEM((plane, HEAD_SIZE), F32),
        ],
        compiler_params=pltpu.CompilerParams(vmem_limit_bytes=VMEM_LIMIT),
        name="local_parts",
    )(query_token_query, query_token_key, query_token_value, document_key, document_value)
    received = lax.all_to_all(send, ("x", "z"), 0, 0, tiled=True)
    send = middle(received, chunk, 2 * width, plane, SIZES[0], False)
    received = lax.all_to_all(send, "y", 0, 0, tiled=True)
    send = middle(received, chunk, 2 * width, SIZES[0], plane, True)
    received = lax.all_to_all(send, ("x", "z"), 0, 0, tiled=True)
    answer_half = pl.pallas_call(
        answer_kernel,
        grid=(1,),
        out_shape=jax.ShapeDtypeStruct(query_token_query.shape, BF16),
        in_specs=[pl.BlockSpec((rows, HEAD_SIZE), lambda i: (0, 2 * width // HEAD_SIZE))],
        out_specs=pl.BlockSpec(query_token_query.shape, lambda i: (0, 0)),
        scratch_shapes=[pltpu.VMEM((rows, HEAD_SIZE), F32)],
        name="answer_rows",
    )(received)
    answer = lax.all_gather(answer_half, "tp", axis=1, tiled=True)
    ctx_out = attend(document_query, received, document_key, document_value)
    return (ctx_out, answer)


def solution(mesh):
    grid = Mesh(mesh.devices.reshape(SIZES + (-1,)), ("y", "x", "z", "tp"))
    blk = ("y", "x", "z")
    placed = (P(blk, "tp"),) * 3 + (P(None, "tp"),) * 3
    return jax.shard_map(
        body, mesh=grid, in_specs=placed, out_specs=(P(blk, "tp"), P()), check_vma=False
    )
```

```python
import math

import jax
import jax.numpy as jnp
from jax import lax
from jax.experimental import pallas as pl
from jax.experimental.pallas import tpu as pltpu
from jax.sharding import Mesh, PartitionSpec as P

HEAD_SIZE = 128
QUERY_PER_KEY = 4
QUERY_TOKENS = 4
SIZES = (8, 4, 8)
NEG = -1e30
F32 = jnp.float32
BF16 = jnp.bfloat16
SCALE = HEAD_SIZE**-0.5
LOG2E = math.log2(math.e)
VMEM_LIMIT = 40 * 1024 * 1024


FACTOR = SCALE * LOG2E


def dot_nt(a, b):
    return lax.dot_general(a, b, (((1,), (1,)), ((), ())), preferred_element_type=F32)


def block_index():
    return (lax.axis_index("y") * SIZES[1] + lax.axis_index("x")) * SIZES[2] + lax.axis_index("z")


def parts_of(value, count):
    terms = []
    for _ in range(count - 1):
        term = value.astype(BF16).astype(F32)
        terms.append(term)
        value = value - term
    return terms + [value]


def record_rows(peak, total, mixed):
    return parts_of(mixed, 2) + parts_of(peak, 3) + parts_of(total, 2)


def merge_records(ref, count, stride):
    row = lambda k: ref[pl.ds(k, count, stride=stride), :]
    mixed = row(0) + row(1)
    peak = (row(2) + row(3)) + row(4)
    total = row(5) + row(6)
    top = jnp.max(peak, axis=0, keepdims=True)
    weight = jnp.exp(peak - top)
    return (
        top,
        jnp.sum(total * weight, axis=0, keepdims=True),
        jnp.sum(mixed * weight, axis=0, keepdims=True),
    )


def local_kernel(
    qt_hbm, qk_hbm, qv_hbm, k_hbm, v_hbm, out_ref, qt_ref, qk_ref, qv_ref, rec_ref, q_ref, sems
):
    half, width = k_hbm.shape[0] // 2, k_hbm.shape[1]
    copies = [
        pltpu.make_async_copy(source, target, sems.at[n])
        for n, (source, target) in enumerate(
            [
                (qt_hbm, qt_ref),
                (k_hbm.at[:half, :], out_ref.at[:, :width]),
                (k_hbm.at[half:, :], out_ref.at[:, width : 2 * width]),
                (v_hbm.at[:half, :], out_ref.at[:, 2 * width : 3 * width]),
                (v_hbm.at[half:, :], out_ref.at[:, 3 * width : 4 * width]),
                (qk_hbm, qk_ref),
                (qv_hbm, qv_ref),
            ]
        )
    ]
    for copy in copies:
        copy.start()
    rec_ref[...] = jnp.zeros_like(rec_ref)
    first_block = block_index() == 0
    for copy in copies:
        copy.wait()
    heads = qt_ref.shape[1] // HEAD_SIZE
    chunk = half // (heads * QUERY_TOKENS)
    for h in range(heads):
        q_ref[h * QUERY_TOKENS : (h + 1) * QUERY_TOKENS, :] = qt_ref[
            :, h * HEAD_SIZE : (h + 1) * HEAD_SIZE
        ].astype(F32)
    group = QUERY_PER_KEY * QUERY_TOKENS
    token = lax.broadcasted_iota(jnp.int32, (group, 1), 0) % QUERY_TOKENS
    for kv in range(heads // QUERY_PER_KEY):
        cols = slice(kv * HEAD_SIZE, (kv + 1) * HEAD_SIZE)
        part = lambda n: out_ref[:, n * width + kv * HEAD_SIZE : n * width + (kv + 1) * HEAD_SIZE]
        q = q_ref[kv * group : (kv + 1) * group, :]
        scores = [dot_nt(q.astype(BF16), part(n)) * SCALE for n in range(2)]
        new_k = qk_ref[:, cols].astype(F32)
        new_v = qv_ref[:, cols].astype(F32)
        own = []
        for j in range(QUERY_TOKENS):
            s = jnp.sum(q * new_k[j : j + 1, :], axis=-1, keepdims=True) * SCALE
            own.append(jnp.where(jnp.logical_and(token >= j, first_block), s, NEG))
        top = jnp.max(jnp.maximum(scores[0], scores[1]), axis=-1, keepdims=True)
        for s in own:
            top = jnp.maximum(top, s)
        expo = [jnp.exp(s - top) for s in scores]
        total = jnp.sum(expo[0] + expo[1], axis=-1, keepdims=True)
        mixed = jnp.dot(expo[0].astype(BF16), part(2), preferred_element_type=F32)
        mixed += jnp.dot(expo[1].astype(BF16), part(3), preferred_element_type=F32)
        for j, s in enumerate(own):
            e = jnp.exp(s - top)
            total = total + e
            mixed = mixed + e.astype(BF16).astype(F32) * new_v[j : j + 1, :]
        full = (group, HEAD_SIZE)
        for k, value in enumerate(
            record_rows(jnp.broadcast_to(top, full), jnp.broadcast_to(total, full), mixed)
        ):
            rec_ref[pl.ds(kv * group * chunk + k, group, stride=chunk), :] = value
    out_ref[:, 4 * width :] = rec_ref[...].astype(BF16)


def local_parts(inputs, rows, width):
    half = rows // 2
    full = 4 * width + HEAD_SIZE
    hbm = pl.BlockSpec(memory_space=pltpu.HBM)
    return pl.pallas_call(
        local_kernel,
        out_shape=jax.ShapeDtypeStruct((half, full), BF16),
        in_specs=[hbm] * len(inputs),
        out_specs=pl.BlockSpec(memory_space=pltpu.VMEM),
        scratch_shapes=[pltpu.VMEM(array.shape, BF16) for array in inputs[:3]]
        + [
            pltpu.VMEM((half, HEAD_SIZE), F32),
            pltpu.VMEM((inputs[0].shape[1] // HEAD_SIZE * QUERY_TOKENS, HEAD_SIZE), F32),
            pltpu.SemaphoreType.DMA((7,)),
        ],
        compiler_params=pltpu.CompilerParams(vmem_limit_bytes=VMEM_LIMIT),
        name="local_parts",
    )(*(pltpu.with_memory_space_constraint(array, pltpu.HBM) for array in inputs))


def middle_kernel(last, rec_in_ref, chunk_ref, out_ref, in_ref, rec_ref):
    chunk, width = chunk_ref.shape
    in_ref[...] = rec_in_ref[...].astype(F32)
    peak, total, mixed = merge_records(in_ref, in_ref.shape[0] // chunk, chunk)
    if last:
        rec_ref[...] = jnp.broadcast_to(mixed / total, rec_ref.shape)
    else:
        rec_ref[...] = jnp.zeros_like(rec_ref)
        for k, value in enumerate(record_rows(peak, total, mixed)):
            rec_ref[k : k + 1, :] = value
    record = rec_ref[...].astype(BF16)
    piece = chunk_ref[...]
    for i in range(out_ref.shape[0] // chunk):
        out_ref[i * chunk : (i + 1) * chunk, :width] = piece
        out_ref[i * chunk : (i + 1) * chunk, width:] = record


def middle(received, chunk, copies, last):
    def kernel(*refs):
        middle_kernel(last, *refs)

    rows, total = received.shape
    width = total - HEAD_SIZE
    return pl.pallas_call(
        kernel,
        grid=(1,),
        out_shape=jax.ShapeDtypeStruct((copies * chunk, total), BF16),
        in_specs=[
            pl.BlockSpec((rows, HEAD_SIZE), lambda i: (0, width // HEAD_SIZE)),
            pl.BlockSpec((chunk, width), lambda i: (0, 0)),
        ],
        out_specs=pl.BlockSpec((copies * chunk, total), lambda i: (0, 0)),
        scratch_shapes=[
            pltpu.VMEM((rows, HEAD_SIZE), F32),
            pltpu.VMEM((chunk, HEAD_SIZE), F32),
        ],
        compiler_params=pltpu.CompilerParams(vmem_limit_bytes=VMEM_LIMIT),
        name="merge_last" if last else "merge_first",
    )(received, received)


def answer_kernel(rec_in_ref, out_ref, in_ref):
    heads = out_ref.shape[1] // HEAD_SIZE
    count = heads * QUERY_TOKENS
    in_ref[...] = rec_in_ref[...].astype(F32)
    found = in_ref[pl.ds(0, count, stride=in_ref.shape[0] // count), :]
    for h in range(heads):
        out_ref[:, h * HEAD_SIZE : (h + 1) * HEAD_SIZE] = found[
            h * QUERY_TOKENS : (h + 1) * QUERY_TOKENS
        ].astype(BF16)


def answer_rows(received, width):
    rows, total = received.shape
    shape = (QUERY_TOKENS, width)
    return pl.pallas_call(
        answer_kernel,
        grid=(1,),
        out_shape=jax.ShapeDtypeStruct(shape, BF16),
        in_specs=[pl.BlockSpec((rows, HEAD_SIZE), lambda i: (0, total // HEAD_SIZE - 1))],
        out_specs=pl.BlockSpec(shape, lambda i: (0, 0)),
        scratch_shapes=[pltpu.VMEM((rows, HEAD_SIZE), F32)],
        compiler_params=pltpu.CompilerParams(vmem_limit_bytes=VMEM_LIMIT),
        name="answer_rows",
    )(received)


def lanes(value):
    return jnp.broadcast_to(value, (value.shape[0], HEAD_SIZE))


def top_of(pieces):
    high = pieces[0]
    for piece in pieces[1:]:
        high = jnp.maximum(high, piece)
    return lanes(jnp.max(high, axis=-1, keepdims=True))


def split(scores):
    return [scores[:, c : c + HEAD_SIZE] for c in range(0, scores.shape[1], HEAD_SIZE)]


def exps(pieces, base):
    return jnp.concatenate([jnp.exp2(p * FACTOR - base).astype(BF16) for p in pieces], axis=1)


def with_ones(values):
    return jnp.concatenate([values, jnp.ones_like(values)], axis=1)


STEP = 256


def attend_kernel(step, ahead, q_ref, kv_ref, k_ref, v_ref, out_hbm, out_ref, sems):
    rows = q_ref.shape[0]
    heads = q_ref.shape[1] // HEAD_SIZE
    heads_kv = heads // QUERY_PER_KEY
    off = jnp.where(block_index() > 0, 0.0, -NEG).astype(F32)
    line = lax.broadcasted_iota(jnp.int32, (step, step), 0)
    column = lax.broadcasted_iota(jnp.int32, (step, step), 1)
    keep = column <= line
    head = lambda n: slice(n * HEAD_SIZE, (n + 1) * HEAD_SIZE)
    far_values = [with_ones(kv_ref[:, head(2 * heads_kv + n)]) for n in range(2 * heads_kv)]
    values = [with_ones(v_ref[:, head(n)]) for n in range(heads_kv)]
    items = [(h, at) for h in range(heads) for at in range(0, rows, step)]
    copies = []

    def scores_of(h, at):
        kv = h // QUERY_PER_KEY
        q = q_ref[at : at + step, head(h)]
        return (
            dot_nt(q, kv_ref[:, head(kv)]),
            dot_nt(q, kv_ref[:, head(heads_kv + kv)]),
            dot_nt(q, k_ref[: at + step, head(kv)]),
        )

    coming = [scores_of(*item) for item in items[:ahead]]
    for n, (h, at) in enumerate(items):
        if n + ahead < len(items):
            coming.append(scores_of(*items[n + ahead]))
        far_0, far_1, near = coming.pop(0)
        kv = h // QUERY_PER_KEY
        end = at + step
        far = [split(far_0), split(far_1)]
        own = split(near[:, :at]) if at else []
        own += split(jnp.where(keep, near[:, at:], NEG))
        peak = jnp.maximum(top_of(far[0] + far[1]) - off, top_of(own))
        base = peak * FACTOR
        both = jnp.dot(exps(own, base), values[kv][:end], preferred_element_type=F32)
        for side in range(2):
            both += jnp.dot(
                exps(far[side], base + off),
                far_values[side * heads_kv + kv],
                preferred_element_type=F32,
            )
        out_ref[at:end, head(h)] = (both[:, :HEAD_SIZE] * (1.0 / both[:, HEAD_SIZE:])).astype(BF16)
        if end == rows:
            copy = pltpu.make_async_copy(
                out_ref.at[:, head(h)], out_hbm.at[:, head(h)], sems.at[h]
            )
            copy.start()
            copies.append(copy)
    for copy in copies:
        copy.wait()


def attend(document_query, received, document_key, document_value, step=STEP, ahead=1):
    shape = document_query.shape
    vmem = pl.BlockSpec(memory_space=pltpu.VMEM)

    def kernel(*refs):
        attend_kernel(step, ahead, *refs)

    return pl.pallas_call(
        kernel,
        out_shape=jax.ShapeDtypeStruct(shape, BF16),
        in_specs=[vmem] * 4,
        out_specs=pl.BlockSpec(memory_space=pltpu.HBM),
        scratch_shapes=[
            pltpu.VMEM(shape, BF16),
            pltpu.SemaphoreType.DMA((shape[1] // HEAD_SIZE,)),
        ],
        compiler_params=pltpu.CompilerParams(vmem_limit_bytes=VMEM_LIMIT),
        name="attend",
    )(document_query, received, document_key, document_value)


def body(
    document_query,
    document_key,
    document_value,
    query_token_query,
    query_token_key,
    query_token_value,
):
    rows, width = document_key.shape
    plane = SIZES[1] * SIZES[2]
    chunk = rows // 2 // plane
    inputs = (query_token_query, query_token_key, query_token_value, document_key, document_value)
    send = local_parts(inputs, rows, width)
    received = lax.all_to_all(send, ("x", "z"), 0, 0, tiled=True)
    send = middle(received, chunk, SIZES[0], False)
    received = lax.all_to_all(send, "y", 0, 0, tiled=True)
    send = middle(received, chunk, plane, True)
    received = lax.all_to_all(send, ("x", "z"), 0, 0, tiled=True)
    answer_half = answer_rows(received, query_token_query.shape[1])
    other_half = lax.ppermute(answer_half, "tp", [(0, 1), (1, 0)])
    ctx_out = attend(document_query, received, document_key, document_value)
    first = lax.axis_index("tp") == 0
    halves = (
        jnp.where(first, answer_half, other_half),
        jnp.where(first, other_half, answer_half),
    )
    return (ctx_out, jnp.concatenate(halves, axis=1))


def solution(mesh):
    grid = Mesh(mesh.devices.reshape(SIZES + (-1,)), ("y", "x", "z", "tp"))
    blk = ("y", "x", "z")
    placed = (P(blk, "tp"),) * 3 + (P(None, "tp"),) * 3
    return jax.shard_map(
        body, mesh=grid, in_specs=placed, out_specs=(P(blk, "tp"), P()), check_vma=False
    )
```

```python
import math

import jax
import jax.numpy as jnp
import numpy as np
from jax import lax
from jax.experimental import pallas as pl
from jax.experimental.pallas import tpu as pltpu
from jax.sharding import Mesh, PartitionSpec as P

HEAD_SIZE = 128
QUERY_PER_KEY = 4
QUERY_TOKENS = 4
SIZES = (8, 4, 8)
NEG = -1e30
F32 = jnp.float32
BF16 = jnp.bfloat16
SCALE = HEAD_SIZE**-0.5
LOG2E = math.log2(math.e)
VMEM_LIMIT = 40 * 1024 * 1024


FACTOR = SCALE * LOG2E


AXES = ("y", "x", "z", "tp")


def exchange_groups():
    ids = np.arange(2 * math.prod(SIZES)).reshape(SIZES + (2,))
    y, x, z = SIZES
    first = np.moveaxis(ids[..., 0], 0, -1).reshape(x * z, y)
    second = ids[..., 1].reshape(y * x, z)
    planes = np.concatenate([first.T, second.T]).tolist()
    lines = np.concatenate([first, second]).tolist()
    return planes, lines


def exchange(array, groups):
    return lax.all_to_all(array, AXES, 0, 0, tiled=True, axis_index_groups=groups)


def dot_nt(a, b):
    return lax.dot_general(a, b, (((1,), (1,)), ((), ())), preferred_element_type=F32)


def block_index():
    return (lax.axis_index("y") * SIZES[1] + lax.axis_index("x")) * SIZES[2] + lax.axis_index("z")


def parts_of(value, count):
    terms = []
    for _ in range(count - 1):
        term = value.astype(BF16).astype(F32)
        terms.append(term)
        value = value - term
    return terms + [value]


def record_rows(peak, total, mixed):
    return parts_of(mixed, 2) + parts_of(peak, 3) + parts_of(total, 2)


def merge_records(ref, count, stride):
    row = lambda k: ref[pl.ds(k, count, stride=stride), :]
    mixed = row(0) + row(1)
    peak = (row(2) + row(3)) + row(4)
    total = row(5) + row(6)
    top = jnp.max(peak, axis=0, keepdims=True)
    weight = jnp.exp(peak - top)
    return (
        top,
        jnp.sum(total * weight, axis=0, keepdims=True),
        jnp.sum(mixed * weight, axis=0, keepdims=True),
    )


def local_kernel(
    qt_hbm, qk_hbm, qv_hbm, k_hbm, v_hbm, out_ref, qt_ref, qk_ref, qv_ref, rec_ref, q_ref, sems
):
    half, width = k_hbm.shape[0] // 2, k_hbm.shape[1]
    copies = [
        pltpu.make_async_copy(source, target, sems.at[n])
        for n, (source, target) in enumerate(
            [
                (qt_hbm, qt_ref),
                (k_hbm.at[:half, :], out_ref.at[:, :width]),
                (k_hbm.at[half:, :], out_ref.at[:, width : 2 * width]),
                (v_hbm.at[:half, :], out_ref.at[:, 2 * width : 3 * width]),
                (v_hbm.at[half:, :], out_ref.at[:, 3 * width : 4 * width]),
                (qk_hbm, qk_ref),
                (qv_hbm, qv_ref),
            ]
        )
    ]
    for copy in copies:
        copy.start()
    rec_ref[...] = jnp.zeros_like(rec_ref)
    first_block = block_index() == 0
    for copy in copies:
        copy.wait()
    heads = qt_ref.shape[1] // HEAD_SIZE
    chunk = half // (heads * QUERY_TOKENS)
    for h in range(heads):
        q_ref[h * QUERY_TOKENS : (h + 1) * QUERY_TOKENS, :] = qt_ref[
            :, h * HEAD_SIZE : (h + 1) * HEAD_SIZE
        ].astype(F32)
    group = QUERY_PER_KEY * QUERY_TOKENS
    token = lax.broadcasted_iota(jnp.int32, (group, 1), 0) % QUERY_TOKENS
    for kv in range(heads // QUERY_PER_KEY):
        cols = slice(kv * HEAD_SIZE, (kv + 1) * HEAD_SIZE)
        part = lambda n: out_ref[:, n * width + kv * HEAD_SIZE : n * width + (kv + 1) * HEAD_SIZE]
        q = q_ref[kv * group : (kv + 1) * group, :]
        scores = [dot_nt(q.astype(BF16), part(n)) * SCALE for n in range(2)]
        new_k = qk_ref[:, cols].astype(F32)
        new_v = qv_ref[:, cols].astype(F32)
        own = []
        for j in range(QUERY_TOKENS):
            s = jnp.sum(q * new_k[j : j + 1, :], axis=-1, keepdims=True) * SCALE
            own.append(jnp.where(jnp.logical_and(token >= j, first_block), s, NEG))
        top = jnp.max(jnp.maximum(scores[0], scores[1]), axis=-1, keepdims=True)
        for s in own:
            top = jnp.maximum(top, s)
        expo = [jnp.exp(s - top) for s in scores]
        total = jnp.sum(expo[0] + expo[1], axis=-1, keepdims=True)
        mixed = jnp.dot(expo[0].astype(BF16), part(2), preferred_element_type=F32)
        mixed += jnp.dot(expo[1].astype(BF16), part(3), preferred_element_type=F32)
        for j, s in enumerate(own):
            e = jnp.exp(s - top)
            total = total + e
            mixed = mixed + e.astype(BF16).astype(F32) * new_v[j : j + 1, :]
        full = (group, HEAD_SIZE)
        for k, value in enumerate(
            record_rows(jnp.broadcast_to(top, full), jnp.broadcast_to(total, full), mixed)
        ):
            rec_ref[pl.ds(kv * group * chunk + k, group, stride=chunk), :] = value
    out_ref[:, 4 * width :] = rec_ref[...].astype(BF16)


def local_parts(inputs, rows, width):
    half = rows // 2
    full = 4 * width + HEAD_SIZE
    hbm = pl.BlockSpec(memory_space=pltpu.HBM)
    return pl.pallas_call(
        local_kernel,
        out_shape=jax.ShapeDtypeStruct((half, full), BF16),
        in_specs=[hbm] * len(inputs),
        out_specs=pl.BlockSpec(memory_space=pltpu.VMEM),
        scratch_shapes=[pltpu.VMEM(array.shape, BF16) for array in inputs[:3]]
        + [
            pltpu.VMEM((half, HEAD_SIZE), F32),
            pltpu.VMEM((inputs[0].shape[1] // HEAD_SIZE * QUERY_TOKENS, HEAD_SIZE), F32),
            pltpu.SemaphoreType.DMA((7,)),
        ],
        compiler_params=pltpu.CompilerParams(vmem_limit_bytes=VMEM_LIMIT),
        name="local_parts",
    )(*(pltpu.with_memory_space_constraint(array, pltpu.HBM) for array in inputs))


def middle_kernel(last, rec_in_ref, chunk_ref, out_ref, in_ref, rec_ref):
    chunk, width = chunk_ref.shape
    in_ref[...] = rec_in_ref[...].astype(F32)
    peak, total, mixed = merge_records(in_ref, in_ref.shape[0] // chunk, chunk)
    if last:
        rec_ref[...] = jnp.broadcast_to(mixed / total, rec_ref.shape)
    else:
        rec_ref[...] = jnp.zeros_like(rec_ref)
        for k, value in enumerate(record_rows(peak, total, mixed)):
            rec_ref[k : k + 1, :] = value
    record = rec_ref[...].astype(BF16)
    piece = chunk_ref[...]
    for i in range(out_ref.shape[0] // chunk):
        out_ref[i * chunk : (i + 1) * chunk, :width] = piece
        out_ref[i * chunk : (i + 1) * chunk, width:] = record


def middle(received, chunk, copies, last):
    def kernel(*refs):
        middle_kernel(last, *refs)

    rows, total = received.shape
    width = total - HEAD_SIZE
    return pl.pallas_call(
        kernel,
        grid=(1,),
        out_shape=jax.ShapeDtypeStruct((copies * chunk, total), BF16),
        in_specs=[
            pl.BlockSpec((rows, HEAD_SIZE), lambda i: (0, width // HEAD_SIZE)),
            pl.BlockSpec((chunk, width), lambda i: (0, 0)),
        ],
        out_specs=pl.BlockSpec((copies * chunk, total), lambda i: (0, 0)),
        scratch_shapes=[
            pltpu.VMEM((rows, HEAD_SIZE), F32),
            pltpu.VMEM((chunk, HEAD_SIZE), F32),
        ],
        compiler_params=pltpu.CompilerParams(vmem_limit_bytes=VMEM_LIMIT),
        name="merge_last" if last else "merge_first",
    )(received, received)


def answer_kernel(rec_in_ref, out_ref, in_ref):
    heads = out_ref.shape[1] // HEAD_SIZE
    count = heads * QUERY_TOKENS
    in_ref[...] = rec_in_ref[...].astype(F32)
    found = in_ref[pl.ds(0, count, stride=in_ref.shape[0] // count), :]
    for h in range(heads):
        out_ref[:, h * HEAD_SIZE : (h + 1) * HEAD_SIZE] = found[
            h * QUERY_TOKENS : (h + 1) * QUERY_TOKENS
        ].astype(BF16)


def answer_rows(received, width):
    rows, total = received.shape
    shape = (QUERY_TOKENS, width)
    return pl.pallas_call(
        answer_kernel,
        grid=(1,),
        out_shape=jax.ShapeDtypeStruct(shape, BF16),
        in_specs=[pl.BlockSpec((rows, HEAD_SIZE), lambda i: (0, total // HEAD_SIZE - 1))],
        out_specs=pl.BlockSpec(shape, lambda i: (0, 0)),
        scratch_shapes=[pltpu.VMEM((rows, HEAD_SIZE), F32)],
        compiler_params=pltpu.CompilerParams(vmem_limit_bytes=VMEM_LIMIT),
        name="answer_rows",
    )(received)


def lanes(value):
    return jnp.broadcast_to(value, (value.shape[0], HEAD_SIZE))


def top_of(pieces):
    high = pieces[0]
    for piece in pieces[1:]:
        high = jnp.maximum(high, piece)
    return lanes(jnp.max(high, axis=-1, keepdims=True))


def split(scores):
    return [scores[:, c : c + HEAD_SIZE] for c in range(0, scores.shape[1], HEAD_SIZE)]


def exps(pieces, base):
    return jnp.concatenate([jnp.exp2(p * FACTOR - base).astype(BF16) for p in pieces], axis=1)


def with_ones(values):
    return jnp.concatenate([values, jnp.ones_like(values)], axis=1)


STEP = 256


def attend_kernel(step, ahead, q_ref, kv_ref, k_ref, v_ref, out_hbm, out_ref, sems):
    rows = q_ref.shape[0]
    heads = q_ref.shape[1] // HEAD_SIZE
    heads_kv = heads // QUERY_PER_KEY
    off = jnp.where(block_index() > 0, 0.0, -NEG).astype(F32)
    line = lax.broadcasted_iota(jnp.int32, (step, step), 0)
    column = lax.broadcasted_iota(jnp.int32, (step, step), 1)
    keep = column <= line
    head = lambda n: slice(n * HEAD_SIZE, (n + 1) * HEAD_SIZE)
    far_values = [with_ones(kv_ref[:, head(2 * heads_kv + n)]) for n in range(2 * heads_kv)]
    values = [with_ones(v_ref[:, head(n)]) for n in range(heads_kv)]
    items = [(h, at) for h in range(heads) for at in range(0, rows, step)]
    copies = []

    def scores_of(h, at):
        kv = h // QUERY_PER_KEY
        q = q_ref[at : at + step, head(h)]
        return (
            dot_nt(q, kv_ref[:, head(kv)]),
            dot_nt(q, kv_ref[:, head(heads_kv + kv)]),
            dot_nt(q, k_ref[: at + step, head(kv)]),
        )

    coming = [scores_of(*item) for item in items[:ahead]]
    for n, (h, at) in enumerate(items):
        if n + ahead < len(items):
            coming.append(scores_of(*items[n + ahead]))
        far_0, far_1, near = coming.pop(0)
        kv = h // QUERY_PER_KEY
        end = at + step
        far = [split(far_0), split(far_1)]
        own = split(near[:, :at]) if at else []
        own += split(jnp.where(keep, near[:, at:], NEG))
        peak = jnp.maximum(top_of(far[0] + far[1]) - off, top_of(own))
        base = peak * FACTOR
        both = jnp.dot(exps(own, base), values[kv][:end], preferred_element_type=F32)
        for side in range(2):
            both += jnp.dot(
                exps(far[side], base + off),
                far_values[side * heads_kv + kv],
                preferred_element_type=F32,
            )
        out_ref[at:end, head(h)] = (both[:, :HEAD_SIZE] * (1.0 / both[:, HEAD_SIZE:])).astype(BF16)
        if end == rows:
            copy = pltpu.make_async_copy(
                out_ref.at[:, head(h)], out_hbm.at[:, head(h)], sems.at[h]
            )
            copy.start()
            copies.append(copy)
    for copy in copies:
        copy.wait()


def attend(document_query, received, document_key, document_value, step=STEP, ahead=1):
    shape = document_query.shape
    vmem = pl.BlockSpec(memory_space=pltpu.VMEM)

    def kernel(*refs):
        attend_kernel(step, ahead, *refs)

    return pl.pallas_call(
        kernel,
        out_shape=jax.ShapeDtypeStruct(shape, BF16),
        in_specs=[vmem] * 4,
        out_specs=pl.BlockSpec(memory_space=pltpu.HBM),
        scratch_shapes=[
            pltpu.VMEM(shape, BF16),
            pltpu.SemaphoreType.DMA((shape[1] // HEAD_SIZE,)),
        ],
        compiler_params=pltpu.CompilerParams(vmem_limit_bytes=VMEM_LIMIT),
        name="attend",
    )(document_query, received, document_key, document_value)


def body(
    document_query,
    document_key,
    document_value,
    query_token_query,
    query_token_key,
    query_token_value,
):
    rows, width = document_key.shape
    planes, lines = exchange_groups()
    plane = len(planes[0])
    chunk = rows // 2 // plane
    inputs = (query_token_query, query_token_key, query_token_value, document_key, document_value)
    send = local_parts(inputs, rows, width)
    received = exchange(send, planes)
    send = middle(received, chunk, len(lines[0]), False)
    received = exchange(send, lines)
    send = middle(received, chunk, plane, True)
    received = exchange(send, planes)
    answer_half = answer_rows(received, query_token_query.shape[1])
    other_half = lax.ppermute(answer_half, "tp", [(0, 1), (1, 0)])
    ctx_out = attend(document_query, received, document_key, document_value)
    first = lax.axis_index("tp") == 0
    halves = (
        jnp.where(first, answer_half, other_half),
        jnp.where(first, other_half, answer_half),
    )
    return (ctx_out, jnp.concatenate(halves, axis=1))


def solution(mesh):
    grid = Mesh(mesh.devices.reshape(SIZES + (-1,)), ("y", "x", "z", "tp"))
    blk = ("y", "x", "z")
    placed = (P(blk, "tp"),) * 3 + (P(None, "tp"),) * 3
    return jax.shard_map(
        body, mesh=grid, in_specs=placed, out_specs=(P(blk, "tp"), P()), check_vma=False
    )
```

```python
import math

import jax
import jax.numpy as jnp
import numpy as np
from jax import lax
from jax.experimental import pallas as pl
from jax.experimental.pallas import tpu as pltpu
from jax.sharding import Mesh, PartitionSpec as P

HEAD_SIZE = 128
QUERY_PER_KEY = 4
QUERY_TOKENS = 4
SIZES = (8, 4, 8)
NEG = -1e30
F32 = jnp.float32
BF16 = jnp.bfloat16
SCALE = HEAD_SIZE**-0.5
LOG2E = math.log2(math.e)
VMEM_LIMIT = 40 * 1024 * 1024


FACTOR = SCALE * LOG2E


AXES = ("y", "x", "z", "tp")


def exchange_groups():
    ids = np.arange(2 * math.prod(SIZES)).reshape(SIZES + (2,))
    y, x, z = SIZES
    first = np.moveaxis(ids[..., 0], 0, -1).reshape(x * z, y)
    second = ids[..., 1].reshape(y * x, z)
    planes = np.concatenate([first.T, second.T]).tolist()
    lines = np.concatenate([first, second]).tolist()
    return planes, lines


def exchange(array, groups):
    return lax.all_to_all(array, AXES, 0, 0, tiled=True, axis_index_groups=groups)


def dot_nt(a, b):
    return lax.dot_general(a, b, (((1,), (1,)), ((), ())), preferred_element_type=F32)


def block_index():
    return (lax.axis_index("y") * SIZES[1] + lax.axis_index("x")) * SIZES[2] + lax.axis_index("z")


def parts_of(value, count):
    terms = []
    for _ in range(count - 1):
        term = value.astype(BF16).astype(F32)
        terms.append(term)
        value = value - term
    return terms + [value]


def record_rows(peak, total, mixed):
    return parts_of(mixed, 2) + parts_of(peak, 3) + parts_of(total, 2)


def merge_records(ref, count, stride):
    row = lambda k: ref[pl.ds(k, count, stride=stride), :]
    mixed = row(0) + row(1)
    peak = (row(2) + row(3)) + row(4)
    total = row(5) + row(6)
    top = jnp.max(peak, axis=0, keepdims=True)
    weight = jnp.exp(peak - top)
    return (
        top,
        jnp.sum(total * weight, axis=0, keepdims=True),
        jnp.sum(mixed * weight, axis=0, keepdims=True),
    )


def local_kernel(
    qt_hbm,
    qk_hbm,
    qv_hbm,
    k_hbm,
    v_hbm,
    out_ref,
    qt_ref,
    qk_ref,
    qv_ref,
    k_ref,
    v_ref,
    rec_ref,
    q_ref,
    sems,
):
    rows, width = k_hbm.shape
    half = rows // 2
    passed = [
        pltpu.make_async_copy(
            k_hbm.at[n * half : (n + 1) * half, :],
            out_ref.at[:, n * width : (n + 1) * width],
            sems.at[n],
        )
        for n in range(2)
    ]
    copies = [
        pltpu.make_async_copy(source, target, sems.at[2 + n])
        for n, (source, target) in enumerate(
            [
                (qt_hbm, qt_ref),
                (k_hbm, k_ref),
                (v_hbm, v_ref),
                (qk_hbm, qk_ref),
                (qv_hbm, qv_ref),
            ]
        )
    ]
    for copy in copies + passed:
        copy.start()
    rec_ref[...] = jnp.zeros_like(rec_ref)
    first_block = block_index() == 0
    for copy in copies:
        copy.wait()
    heads = qt_ref.shape[1] // HEAD_SIZE
    chunk = half // (heads * QUERY_TOKENS)
    for h in range(heads):
        q_ref[h * QUERY_TOKENS : (h + 1) * QUERY_TOKENS, :] = qt_ref[
            :, h * HEAD_SIZE : (h + 1) * HEAD_SIZE
        ].astype(F32)
    group = QUERY_PER_KEY * QUERY_TOKENS
    token = lax.broadcasted_iota(jnp.int32, (group, 1), 0) % QUERY_TOKENS
    for kv in range(heads // QUERY_PER_KEY):
        cols = slice(kv * HEAD_SIZE, (kv + 1) * HEAD_SIZE)
        q = q_ref[kv * group : (kv + 1) * group, :]
        scores = dot_nt(q.astype(BF16), k_ref[:, cols]) * SCALE
        new_k = qk_ref[:, cols].astype(F32)
        new_v = qv_ref[:, cols].astype(F32)
        own = []
        for j in range(QUERY_TOKENS):
            s = jnp.sum(q * new_k[j : j + 1, :], axis=-1, keepdims=True) * SCALE
            own.append(jnp.where(jnp.logical_and(token >= j, first_block), s, NEG))
        top = jnp.max(scores, axis=-1, keepdims=True)
        for s in own:
            top = jnp.maximum(top, s)
        expo = jnp.exp(scores - top)
        total = jnp.sum(expo, axis=-1, keepdims=True)
        mixed = jnp.dot(expo.astype(BF16), v_ref[:, cols], preferred_element_type=F32)
        for j, s in enumerate(own):
            e = jnp.exp(s - top)
            total = total + e
            mixed = mixed + e.astype(BF16).astype(F32) * new_v[j : j + 1, :]
        full = (group, HEAD_SIZE)
        for k, value in enumerate(
            record_rows(jnp.broadcast_to(top, full), jnp.broadcast_to(total, full), mixed)
        ):
            rec_ref[pl.ds(kv * group * chunk + k, group, stride=chunk), :] = value
    out_ref[:, 2 * width :] = rec_ref[...].astype(BF16)
    for copy in passed:
        copy.wait()


def local_parts(inputs):
    rows, width = inputs[3].shape
    half = rows // 2
    hbm = pl.BlockSpec(memory_space=pltpu.HBM)
    return pl.pallas_call(
        local_kernel,
        out_shape=jax.ShapeDtypeStruct((half, 2 * width + HEAD_SIZE), BF16),
        in_specs=[hbm] * len(inputs),
        out_specs=pl.BlockSpec(memory_space=pltpu.VMEM),
        scratch_shapes=[pltpu.VMEM(array.shape, BF16) for array in inputs]
        + [
            pltpu.VMEM((half, HEAD_SIZE), F32),
            pltpu.VMEM((inputs[0].shape[1] // HEAD_SIZE * QUERY_TOKENS, HEAD_SIZE), F32),
            pltpu.SemaphoreType.DMA((7,)),
        ],
        compiler_params=pltpu.CompilerParams(vmem_limit_bytes=VMEM_LIMIT),
        name="local_parts",
    )(*(pltpu.with_memory_space_constraint(array, pltpu.HBM) for array in inputs))


def passing_on(send, moved, helpers):
    rows, width = moved.shape
    half = rows // 2

    def kernel(send_ref, moved_ref, out_ref):
        position = block_index() * 2 + lax.axis_index("tp")

        @pl.when(jnp.logical_or(position == helpers[0], position == helpers[1]))
        def _():
            for n in range(2):
                out_ref[:, n * width : (n + 1) * width] = moved_ref[n * half : (n + 1) * half, :]

    vmem = pl.BlockSpec(memory_space=pltpu.VMEM)
    return pl.pallas_call(
        kernel,
        out_shape=jax.ShapeDtypeStruct(send.shape, BF16),
        in_specs=[vmem] * 2,
        out_specs=vmem,
        input_output_aliases={0: 0},
        compiler_params=pltpu.CompilerParams(vmem_limit_bytes=VMEM_LIMIT),
        name="passing_on",
    )(send, moved)


def middle_kernel(chunk, rec_in_ref, piece_ref, out_ref, in_ref, rec_ref):
    last = piece_ref.shape[0] == chunk
    in_ref[...] = rec_in_ref[...].astype(F32)
    peak, total, mixed = merge_records(in_ref, in_ref.shape[0] // chunk, chunk)
    if last:
        rec_ref[...] = jnp.broadcast_to(mixed / total, rec_ref.shape)
    else:
        rec_ref[...] = jnp.zeros_like(rec_ref)
        for k, value in enumerate(record_rows(peak, total, mixed)):
            rec_ref[k : k + 1, :] = value
    record = rec_ref[...].astype(BF16)
    width = piece_ref.shape[1]
    for n in range(piece_ref.shape[0] // chunk):
        piece = piece_ref[n * chunk : (n + 1) * chunk, :]
        for at in range(0, out_ref.shape[0], chunk):
            out_ref[at : at + chunk, n * width : (n + 1) * width] = piece
    for at in range(0, out_ref.shape[0], chunk):
        out_ref[at : at + chunk, out_ref.shape[1] - HEAD_SIZE :] = record


def middle(received, chunk, copies, last):
    def kernel(*refs):
        middle_kernel(chunk, *refs)

    rows, total = received.shape
    width = total - HEAD_SIZE
    sources = 1 if last else 2
    shape = (copies * chunk, sources * width + HEAD_SIZE)
    return pl.pallas_call(
        kernel,
        grid=(1,),
        out_shape=jax.ShapeDtypeStruct(shape, BF16),
        in_specs=[
            pl.BlockSpec((rows, HEAD_SIZE), lambda i: (0, width // HEAD_SIZE)),
            pl.BlockSpec((sources * chunk, width), lambda i: (0, 0)),
        ],
        out_specs=pl.BlockSpec(shape, lambda i: (0, 0)),
        scratch_shapes=[
            pltpu.VMEM((rows, HEAD_SIZE), F32),
            pltpu.VMEM((chunk, HEAD_SIZE), F32),
        ],
        compiler_params=pltpu.CompilerParams(vmem_limit_bytes=VMEM_LIMIT),
        name="merge_last" if last else "merge_first",
    )(received, received)


def answer_kernel(rec_in_ref, out_ref, in_ref):
    heads = out_ref.shape[1] // HEAD_SIZE
    count = heads * QUERY_TOKENS
    in_ref[...] = rec_in_ref[...].astype(F32)
    found = in_ref[pl.ds(0, count, stride=in_ref.shape[0] // count), :]
    for h in range(heads):
        out_ref[:, h * HEAD_SIZE : (h + 1) * HEAD_SIZE] = found[
            h * QUERY_TOKENS : (h + 1) * QUERY_TOKENS
        ].astype(BF16)


def answer_rows(received, width):
    rows, total = received.shape
    shape = (QUERY_TOKENS, width)
    return pl.pallas_call(
        answer_kernel,
        grid=(1,),
        out_shape=jax.ShapeDtypeStruct(shape, BF16),
        in_specs=[pl.BlockSpec((rows, HEAD_SIZE), lambda i: (0, total // HEAD_SIZE - 1))],
        out_specs=pl.BlockSpec(shape, lambda i: (0, 0)),
        scratch_shapes=[pltpu.VMEM((rows, HEAD_SIZE), F32)],
        compiler_params=pltpu.CompilerParams(vmem_limit_bytes=VMEM_LIMIT),
        name="answer_rows",
    )(received)


def lanes(value):
    return jnp.broadcast_to(value, (value.shape[0], HEAD_SIZE))


def top_of(pieces):
    high = pieces[0]
    for piece in pieces[1:]:
        high = jnp.maximum(high, piece)
    return lanes(jnp.max(high, axis=-1, keepdims=True))


def split(scores):
    return [scores[:, c : c + HEAD_SIZE] for c in range(0, scores.shape[1], HEAD_SIZE)]


def exps(pieces, base):
    return jnp.concatenate([jnp.exp2(p * FACTOR - base).astype(BF16) for p in pieces], axis=1)


def with_ones(values):
    return jnp.concatenate([values, jnp.ones_like(values)], axis=1)


STEP = 256


def attend_kernel(step, ahead, q_ref, kv_ref, k_ref, v_ref, out_hbm, out_ref, sems):
    rows = q_ref.shape[0]
    heads = q_ref.shape[1] // HEAD_SIZE
    heads_kv = heads // QUERY_PER_KEY
    off = jnp.where(block_index() > 0, 0.0, -NEG).astype(F32)
    line = lax.broadcasted_iota(jnp.int32, (step, step), 0)
    column = lax.broadcasted_iota(jnp.int32, (step, step), 1)
    keep = column <= line
    head = lambda n: slice(n * HEAD_SIZE, (n + 1) * HEAD_SIZE)
    far_values = [with_ones(kv_ref[:, head(2 * heads_kv + n)]) for n in range(2 * heads_kv)]
    values = [with_ones(v_ref[:, head(n)]) for n in range(heads_kv)]
    items = [(h, at) for h in range(heads) for at in range(0, rows, step)]
    copies = []

    def scores_of(h, at):
        kv = h // QUERY_PER_KEY
        q = q_ref[at : at + step, head(h)]
        return (
            dot_nt(q, kv_ref[:, head(kv)]),
            dot_nt(q, kv_ref[:, head(heads_kv + kv)]),
            dot_nt(q, k_ref[: at + step, head(kv)]),
        )

    coming = [scores_of(*item) for item in items[:ahead]]
    for n, (h, at) in enumerate(items):
        if n + ahead < len(items):
            coming.append(scores_of(*items[n + ahead]))
        far_0, far_1, near = coming.pop(0)
        kv = h // QUERY_PER_KEY
        end = at + step
        far = [split(far_0), split(far_1)]
        own = split(near[:, :at]) if at else []
        own += split(jnp.where(keep, near[:, at:], NEG))
        peak = jnp.maximum(top_of(far[0] + far[1]) - off, top_of(own))
        base = peak * FACTOR
        both = jnp.dot(exps(own, base), values[kv][:end], preferred_element_type=F32)
        for side in range(2):
            both += jnp.dot(
                exps(far[side], base + off),
                far_values[side * heads_kv + kv],
                preferred_element_type=F32,
            )
        out_ref[at:end, head(h)] = (both[:, :HEAD_SIZE] * (1.0 / both[:, HEAD_SIZE:])).astype(BF16)
        copy = pltpu.make_async_copy(
            out_ref.at[at:end, head(h)], out_hbm.at[at:end, head(h)], sems.at[n]
        )
        copy.start()
        copies.append(copy)
    for copy in copies:
        copy.wait()


def attend(document_query, received, document_key, document_value, step=STEP, ahead=1):
    shape = document_query.shape
    vmem = pl.BlockSpec(memory_space=pltpu.VMEM)

    def kernel(*refs):
        attend_kernel(step, ahead, *refs)

    return pl.pallas_call(
        kernel,
        out_shape=jax.ShapeDtypeStruct(shape, BF16),
        in_specs=[vmem] * 4,
        out_specs=pl.BlockSpec(memory_space=pltpu.HBM),
        scratch_shapes=[
            pltpu.VMEM(shape, BF16),
            pltpu.SemaphoreType.DMA((shape[1] // HEAD_SIZE * shape[0] // step,)),
        ],
        compiler_params=pltpu.CompilerParams(vmem_limit_bytes=VMEM_LIMIT),
        name="attend",
    )(document_query, received, document_key, document_value)


def body(
    document_query,
    document_key,
    document_value,
    query_token_query,
    query_token_key,
    query_token_value,
):
    rows, width = document_key.shape
    planes, lines = exchange_groups()
    plane = len(planes[0])
    chunk = rows // 2 // plane
    roots = [planes[0][0], planes[-SIZES[2]][0]]
    helpers = [planes[0][1], planes[-SIZES[2]][1]]
    moved = lax.ppermute(document_value, AXES, list(zip(roots, helpers)))
    inputs = (
        query_token_query,
        query_token_key,
        query_token_value,
        document_key,
        document_value,
    )
    send = passing_on(local_parts(inputs), moved, helpers)
    received = exchange(send, planes)
    send = middle(received, chunk, len(lines[0]), False)
    received = exchange(send, lines)
    send = middle(received, chunk, plane, True)
    received = exchange(send, planes)
    answer_half = answer_rows(received, query_token_query.shape[1])
    other_half = lax.ppermute(answer_half, "tp", [(0, 1), (1, 0)])
    ctx_out = attend(document_query, received, document_key, document_value)
    first = lax.axis_index("tp") == 0
    halves = (
        jnp.where(first, answer_half, other_half),
        jnp.where(first, other_half, answer_half),
    )
    return (ctx_out, jnp.concatenate(halves, axis=1))


def solution(mesh):
    grid = Mesh(mesh.devices.reshape(SIZES + (-1,)), ("y", "x", "z", "tp"))
    blk = ("y", "x", "z")
    placed = (P(blk, "tp"),) * 3 + (P(None, "tp"),) * 3
    return jax.shard_map(
        body, mesh=grid, in_specs=placed, out_specs=(P(blk, "tp"), P()), check_vma=False
    )
```

```python
import math

import jax
import jax.numpy as jnp
import numpy as np
from jax import lax
from jax.experimental import pallas as pl
from jax.experimental.pallas import tpu as pltpu
from jax.sharding import Mesh, PartitionSpec as P

HEAD_SIZE = 128
QUERY_PER_KEY = 4
QUERY_TOKENS = 4
SIZES = (8, 4, 8)
NEG = -1e30
F32 = jnp.float32
BF16 = jnp.bfloat16
SCALE = HEAD_SIZE**-0.5
LOG2E = math.log2(math.e)
VMEM_LIMIT = 40 * 1024 * 1024


FACTOR = SCALE * LOG2E


AXES = ("y", "x", "z", "tp")


def exchange_groups():
    ids = np.arange(2 * math.prod(SIZES)).reshape(SIZES + (2,))
    y, x, z = SIZES
    first = ids[..., 0].reshape(y * x, z)
    second = np.moveaxis(ids[..., 1], 0, -1).reshape(x * z, y)
    planes = np.concatenate([first.T, second.T]).tolist()
    lines = np.concatenate([first, second]).tolist()
    return planes, lines, (planes[0], planes[z])


def exchange(array, groups):
    return lax.all_to_all(array, AXES, 0, 0, tiled=True, axis_index_groups=groups)


def dot_nt(a, b):
    return lax.dot_general(a, b, (((1,), (1,)), ((), ())), preferred_element_type=F32)


def block_index():
    return (lax.axis_index("y") * SIZES[1] + lax.axis_index("x")) * SIZES[2] + lax.axis_index("z")


def parts_of(value, count):
    terms = []
    for _ in range(count - 1):
        term = value.astype(BF16).astype(F32)
        terms.append(term)
        value = value - term
    return terms + [value]


def record_rows(peak, total, mixed):
    return parts_of(mixed, 2) + parts_of(peak, 3) + parts_of(total, 2)


def merge_records(ref, count, stride):
    row = lambda k: ref[pl.ds(k, count, stride=stride), :]
    mixed = row(0) + row(1)
    peak = (row(2) + row(3)) + row(4)
    total = row(5) + row(6)
    top = jnp.max(peak, axis=0, keepdims=True)
    weight = jnp.exp(peak - top)
    return (
        top,
        jnp.sum(total * weight, axis=0, keepdims=True),
        jnp.sum(mixed * weight, axis=0, keepdims=True),
    )


def local_kernel(
    qt_hbm,
    qk_hbm,
    qv_hbm,
    k_hbm,
    v_hbm,
    out_ref,
    qt_ref,
    qk_ref,
    qv_ref,
    k_ref,
    v_ref,
    rec_ref,
    q_ref,
    sems,
):
    rows, width = k_hbm.shape
    half = rows // 2
    passed = [
        pltpu.make_async_copy(
            k_hbm.at[n * half : (n + 1) * half, :],
            out_ref.at[:, n * width : (n + 1) * width],
            sems.at[n],
        )
        for n in range(2)
    ]
    copies = [
        pltpu.make_async_copy(source, target, sems.at[2 + n])
        for n, (source, target) in enumerate(
            [
                (qt_hbm, qt_ref),
                (k_hbm, k_ref),
                (v_hbm, v_ref),
                (qk_hbm, qk_ref),
                (qv_hbm, qv_ref),
            ]
        )
    ]
    for copy in copies + passed:
        copy.start()
    rec_ref[...] = jnp.zeros_like(rec_ref)
    first_block = block_index() == 0
    qt_copy, k_copy, v_copy, qk_copy, qv_copy = copies
    for copy in (qt_copy, qk_copy, qv_copy):
        copy.wait()
    heads = qt_ref.shape[1] // HEAD_SIZE
    chunk = half // (heads * QUERY_TOKENS)
    for h in range(heads):
        q_ref[h * QUERY_TOKENS : (h + 1) * QUERY_TOKENS, :] = qt_ref[
            :, h * HEAD_SIZE : (h + 1) * HEAD_SIZE
        ].astype(F32)
    group = QUERY_PER_KEY * QUERY_TOKENS
    token = lax.broadcasted_iota(jnp.int32, (group, 1), 0) % QUERY_TOKENS
    groups = range(heads // QUERY_PER_KEY)
    cols = [slice(kv * HEAD_SIZE, (kv + 1) * HEAD_SIZE) for kv in groups]
    queries = [q_ref[kv * group : (kv + 1) * group, :] for kv in groups]
    own = []
    for kv in groups:
        new_k = qk_ref[:, cols[kv]].astype(F32)
        own.append([])
        for j in range(QUERY_TOKENS):
            s = jnp.sum(queries[kv] * new_k[j : j + 1, :], axis=-1, keepdims=True) * SCALE
            own[kv].append(jnp.where(jnp.logical_and(token >= j, first_block), s, NEG))
    k_copy.wait()
    scores = [dot_nt(queries[kv].astype(BF16), k_ref[:, cols[kv]]) * SCALE for kv in groups]
    tops = []
    for kv in groups:
        top = jnp.max(scores[kv], axis=-1, keepdims=True)
        for s in own[kv]:
            top = jnp.maximum(top, s)
        tops.append(top)
    expo = [jnp.exp(scores[kv] - tops[kv]) for kv in groups]
    v_copy.wait()
    mixes = [
        jnp.dot(expo[kv].astype(BF16), v_ref[:, cols[kv]], preferred_element_type=F32)
        for kv in groups
    ]
    full = (group, HEAD_SIZE)
    for kv in groups:
        new_v = qv_ref[:, cols[kv]].astype(F32)
        total = jnp.sum(expo[kv], axis=-1, keepdims=True)
        mixed = mixes[kv]
        for j, s in enumerate(own[kv]):
            e = jnp.exp(s - tops[kv])
            total = total + e
            mixed = mixed + e.astype(BF16).astype(F32) * new_v[j : j + 1, :]
        for k, value in enumerate(
            record_rows(jnp.broadcast_to(tops[kv], full), jnp.broadcast_to(total, full), mixed)
        ):
            rec_ref[pl.ds(kv * group * chunk + k, group, stride=chunk), :] = value
    out_ref[:, 2 * width :] = rec_ref[...].astype(BF16)
    for copy in passed:
        copy.wait()


def local_parts(inputs):
    rows, width = inputs[3].shape
    half = rows // 2
    hbm = pl.BlockSpec(memory_space=pltpu.HBM)
    return pl.pallas_call(
        local_kernel,
        out_shape=jax.ShapeDtypeStruct((half, 2 * width + HEAD_SIZE), BF16),
        in_specs=[hbm] * len(inputs),
        out_specs=pl.BlockSpec(memory_space=pltpu.VMEM),
        scratch_shapes=[pltpu.VMEM(array.shape, BF16) for array in inputs]
        + [
            pltpu.VMEM((half, HEAD_SIZE), F32),
            pltpu.VMEM((inputs[0].shape[1] // HEAD_SIZE * QUERY_TOKENS, HEAD_SIZE), F32),
            pltpu.SemaphoreType.DMA((7,)),
        ],
        compiler_params=pltpu.CompilerParams(vmem_limit_bytes=VMEM_LIMIT),
        name="local_parts",
    )(*(pltpu.with_memory_space_constraint(array, pltpu.HBM) for array in inputs))


def passing_on(send, moved, helpers):
    rows, width = moved.shape
    half = rows // 2

    def kernel(send_ref, moved_ref, out_ref):
        position = block_index() * 2 + lax.axis_index("tp")

        @pl.when(jnp.logical_or(position == helpers[0], position == helpers[1]))
        def _():
            for n in range(2):
                out_ref[:, n * width : (n + 1) * width] = moved_ref[n * half : (n + 1) * half, :]

    vmem = pl.BlockSpec(memory_space=pltpu.VMEM)
    return pl.pallas_call(
        kernel,
        out_shape=jax.ShapeDtypeStruct(send.shape, BF16),
        in_specs=[vmem] * 2,
        out_specs=vmem,
        input_output_aliases={0: 0},
        compiler_params=pltpu.CompilerParams(vmem_limit_bytes=VMEM_LIMIT),
        name="passing_on",
    )(send, moved)


def middle_kernel(chunk, rec_in_ref, piece_ref, out_ref, in_ref, rec_ref):
    last = piece_ref.shape[0] == chunk
    in_ref[...] = rec_in_ref[...].astype(F32)
    peak, total, mixed = merge_records(in_ref, in_ref.shape[0] // chunk, chunk)
    if last:
        rec_ref[...] = jnp.broadcast_to(mixed / total, rec_ref.shape)
    else:
        rec_ref[...] = jnp.zeros_like(rec_ref)
        for k, value in enumerate(record_rows(peak, total, mixed)):
            rec_ref[k : k + 1, :] = value
    record = rec_ref[...].astype(BF16)
    width = piece_ref.shape[1]
    for n in range(piece_ref.shape[0] // chunk):
        piece = piece_ref[n * chunk : (n + 1) * chunk, :]
        for at in range(0, out_ref.shape[0], chunk):
            out_ref[at : at + chunk, n * width : (n + 1) * width] = piece
    for at in range(0, out_ref.shape[0], chunk):
        out_ref[at : at + chunk, out_ref.shape[1] - HEAD_SIZE :] = record


def middle(received, chunk, copies, last):
    def kernel(*refs):
        middle_kernel(chunk, *refs)

    rows, total = received.shape
    width = total - HEAD_SIZE
    sources = 1 if last else 2
    shape = (copies * chunk, sources * width + HEAD_SIZE)
    return pl.pallas_call(
        kernel,
        grid=(1,),
        out_shape=jax.ShapeDtypeStruct(shape, BF16),
        in_specs=[
            pl.BlockSpec((rows, HEAD_SIZE), lambda i: (0, width // HEAD_SIZE)),
            pl.BlockSpec((sources * chunk, width), lambda i: (0, 0)),
        ],
        out_specs=pl.BlockSpec(shape, lambda i: (0, 0)),
        scratch_shapes=[
            pltpu.VMEM((rows, HEAD_SIZE), F32),
            pltpu.VMEM((chunk, HEAD_SIZE), F32),
        ],
        compiler_params=pltpu.CompilerParams(vmem_limit_bytes=VMEM_LIMIT),
        name="merge_last" if last else "merge_first",
    )(received, received)


def answer_kernel(rec_in_ref, out_ref, in_ref):
    heads = out_ref.shape[1] // HEAD_SIZE
    count = heads * QUERY_TOKENS
    in_ref[...] = rec_in_ref[...].astype(F32)
    found = in_ref[pl.ds(0, count, stride=in_ref.shape[0] // count), :]
    for h in range(heads):
        out_ref[:, h * HEAD_SIZE : (h + 1) * HEAD_SIZE] = found[
            h * QUERY_TOKENS : (h + 1) * QUERY_TOKENS
        ].astype(BF16)


def answer_rows(received, width):
    rows, total = received.shape
    shape = (QUERY_TOKENS, width)
    return pl.pallas_call(
        answer_kernel,
        grid=(1,),
        out_shape=jax.ShapeDtypeStruct(shape, BF16),
        in_specs=[pl.BlockSpec((rows, HEAD_SIZE), lambda i: (0, total // HEAD_SIZE - 1))],
        out_specs=pl.BlockSpec(shape, lambda i: (0, 0)),
        scratch_shapes=[pltpu.VMEM((rows, HEAD_SIZE), F32)],
        compiler_params=pltpu.CompilerParams(vmem_limit_bytes=VMEM_LIMIT),
        name="answer_rows",
    )(received)


def lanes(value):
    return jnp.broadcast_to(value, (value.shape[0], HEAD_SIZE))


def top_of(pieces):
    high = pieces[0]
    for piece in pieces[1:]:
        high = jnp.maximum(high, piece)
    return lanes(jnp.max(high, axis=-1, keepdims=True))


def split(scores):
    return [scores[:, c : c + HEAD_SIZE] for c in range(0, scores.shape[1], HEAD_SIZE)]


def exps(pieces, base):
    return jnp.concatenate([jnp.exp2(p * FACTOR - base).astype(BF16) for p in pieces], axis=1)


def with_ones(values):
    return jnp.concatenate([values, jnp.ones_like(values)], axis=1)


STEP = 256


def attend_all(step, ahead, q_ref, kv_ref, k_ref, v_ref, out_hbm, out_ref, sems):
    rows = q_ref.shape[0]
    heads = q_ref.shape[1] // HEAD_SIZE
    heads_kv = heads // QUERY_PER_KEY
    off = jnp.where(block_index() > 0, 0.0, -NEG).astype(F32)
    line = lax.broadcasted_iota(jnp.int32, (step, step), 0)
    column = lax.broadcasted_iota(jnp.int32, (step, step), 1)
    keep = column <= line
    head = lambda n: slice(n * HEAD_SIZE, (n + 1) * HEAD_SIZE)
    far_values = [with_ones(kv_ref[:, head(2 * heads_kv + n)]) for n in range(2 * heads_kv)]
    values = [with_ones(v_ref[:, head(n)]) for n in range(heads_kv)]
    items = [(h, at) for h in range(heads) for at in range(0, rows, step)]
    copies = []

    def scores_of(h, at):
        kv = h // QUERY_PER_KEY
        q = q_ref[at : at + step, head(h)]
        return (
            dot_nt(q, kv_ref[:, head(kv)]),
            dot_nt(q, kv_ref[:, head(heads_kv + kv)]),
            dot_nt(q, k_ref[: at + step, head(kv)]),
        )

    coming = [scores_of(*item) for item in items[:ahead]]
    for n, (h, at) in enumerate(items):
        if n + ahead < len(items):
            coming.append(scores_of(*items[n + ahead]))
        far_0, far_1, near = coming.pop(0)
        kv = h // QUERY_PER_KEY
        end = at + step
        far = [split(far_0), split(far_1)]
        own = split(near[:, :at]) if at else []
        own += split(jnp.where(keep, near[:, at:], NEG))
        peak = jnp.maximum(top_of(far[0] + far[1]) - off, top_of(own))
        base = peak * FACTOR
        both = jnp.dot(exps(own, base), values[kv][:end], preferred_element_type=F32)
        for side in range(2):
            both += jnp.dot(
                exps(far[side], base + off),
                far_values[side * heads_kv + kv],
                preferred_element_type=F32,
            )
        out_ref[at:end, head(h)] = (both[:, :HEAD_SIZE] * (1.0 / both[:, HEAD_SIZE:])).astype(BF16)
        copy = pltpu.make_async_copy(
            out_ref.at[at:end, head(h)], out_hbm.at[at:end, head(h)], sems.at[n]
        )
        copy.start()
        copies.append(copy)
    for copy in copies:
        copy.wait()


def attend(inputs, side, carried, arrived=(), step=STEP, ahead=1):
    shape = inputs[0].shape
    vmem = pl.BlockSpec(memory_space=pltpu.VMEM)
    hbm = pl.BlockSpec(memory_space=pltpu.HBM)
    first = side == 1

    def kernel(*refs):
        ctx_hbm = refs[5 + len(arrived)]
        if first:
            refs[6 + len(arrived)][...] = refs[4][...]

        @pl.when(lax.axis_index("tp") == side)
        def _():
            attend_all(step, ahead, *refs[:4], ctx_hbm, *refs[-2:])

    ctx = jax.ShapeDtypeStruct(shape, BF16)
    return pl.pallas_call(
        kernel,
        out_shape=(ctx, jax.ShapeDtypeStruct(carried.shape, BF16)) if first else (ctx,),
        in_specs=[vmem] * 4 + [vmem if first else hbm] + [vmem] * len(arrived),
        out_specs=(hbm, vmem) if first else (hbm,),
        input_output_aliases={} if first else {4: 0},
        scratch_shapes=[
            pltpu.VMEM(shape, BF16),
            pltpu.SemaphoreType.DMA((shape[1] // HEAD_SIZE * shape[0] // step,)),
        ],
        compiler_params=pltpu.CompilerParams(vmem_limit_bytes=VMEM_LIMIT),
        name="attend_tp1" if first else "attend_tp0",
    )(*inputs, carried, *arrived)


def body(
    document_query,
    document_key,
    document_value,
    query_token_query,
    query_token_key,
    query_token_value,
):
    rows, width = document_key.shape
    planes, lines, root_planes = exchange_groups()
    peers = len(planes[0])
    chunk = rows // 2 // peers
    helpers = [plane[1] for plane in root_planes]
    moved = lax.ppermute(document_value, AXES, [tuple(plane[:2]) for plane in root_planes])
    inputs = (
        query_token_query,
        query_token_key,
        query_token_value,
        document_key,
        document_value,
    )
    send = passing_on(local_parts(inputs), moved, helpers)
    received = exchange(send, planes)
    send = middle(received, chunk, len(lines[0]), False)
    received = exchange(send, lines)
    send = middle(received, chunk, peers, True)
    received = exchange(send, planes)
    answer_half = answer_rows(received, query_token_query.shape[1])
    from_first = lax.ppermute(answer_half, "tp", [(0, 1)])
    inputs = (document_query, received, document_key, document_value)
    ctx_out, sent_half = attend(inputs, 1, answer_half)
    from_second = lax.ppermute(sent_half, "tp", [(1, 0)])
    (ctx_out,) = attend(inputs, 0, ctx_out, (from_first,))
    first = lax.axis_index("tp") == 0
    halves = (
        jnp.where(first, answer_half, from_first),
        jnp.where(first, from_second, answer_half),
    )
    return (ctx_out, jnp.concatenate(halves, axis=1))


def solution(mesh):
    grid = Mesh(mesh.devices.reshape(SIZES + (-1,)), ("y", "x", "z", "tp"))
    blk = ("y", "x", "z")
    placed = (P(blk, "tp"),) * 3 + (P(None, "tp"),) * 3
    return jax.shard_map(
        body, mesh=grid, in_specs=placed, out_specs=(P(blk, "tp"), P()), check_vma=False
    )
```

```python
import math

import jax
import jax.numpy as jnp
import numpy as np
from jax import lax
from jax.experimental import pallas as pl
from jax.experimental.pallas import tpu as pltpu
from jax.sharding import Mesh, PartitionSpec as P

HEAD_SIZE = 128
QUERY_PER_KEY = 4
QUERY_TOKENS = 4
SIZES = (8, 4, 8)
NEG = -1e30
F32 = jnp.float32
BF16 = jnp.bfloat16
SCALE = HEAD_SIZE**-0.5
LOG2E = math.log2(math.e)
VMEM_LIMIT = 40 * 1024 * 1024


FACTOR = SCALE * LOG2E


AXES = ("y", "x", "z", "tp")


def exchange_groups():
    ids = np.arange(2 * math.prod(SIZES)).reshape(SIZES + (2,))
    y, x, z = SIZES
    first = ids[..., 0].reshape(y * x, z)
    second = np.moveaxis(ids[..., 1], 0, -1).reshape(x * z, y)
    planes = np.concatenate([first.T, second.T]).tolist()
    lines = np.concatenate([first, second]).tolist()
    return planes, lines, (planes[0], planes[z])


def exchange(array, groups):
    return lax.all_to_all(array, AXES, 0, 0, tiled=True, axis_index_groups=groups)


def dot_nt(a, b):
    return lax.dot_general(a, b, (((1,), (1,)), ((), ())), preferred_element_type=F32)


def block_index():
    return (lax.axis_index("y") * SIZES[1] + lax.axis_index("x")) * SIZES[2] + lax.axis_index("z")


def parts_of(value, count):
    terms = []
    for _ in range(count - 1):
        term = value.astype(BF16).astype(F32)
        terms.append(term)
        value = value - term
    return terms + [value]


def record_rows(peak, total, mixed):
    return parts_of(mixed, 2) + parts_of(peak, 3) + parts_of(total, 2)


def merge_records(ref, count, stride):
    row = lambda k: ref[pl.ds(k, count, stride=stride), :]
    mixed = row(0) + row(1)
    peak = (row(2) + row(3)) + row(4)
    total = row(5) + row(6)
    top = jnp.max(peak, axis=0, keepdims=True)
    weight = jnp.exp(peak - top)
    return (
        top,
        jnp.sum(total * weight, axis=0, keepdims=True),
        jnp.sum(mixed * weight, axis=0, keepdims=True),
    )


def local_kernel(
    qt_hbm,
    qk_hbm,
    qv_hbm,
    k_hbm,
    v_hbm,
    out_ref,
    qt_ref,
    qk_ref,
    qv_ref,
    k_ref,
    v_ref,
    rec_ref,
    q_ref,
    sems,
):
    rows, width = k_hbm.shape
    half = rows // 2
    passed = [
        pltpu.make_async_copy(
            k_hbm.at[n * half : (n + 1) * half, :],
            out_ref.at[:, n * width : (n + 1) * width],
            sems.at[n],
        )
        for n in range(2)
    ]
    copies = [
        pltpu.make_async_copy(source, target, sems.at[2 + n])
        for n, (source, target) in enumerate(
            [
                (qt_hbm, qt_ref),
                (k_hbm, k_ref),
                (v_hbm, v_ref),
                (qk_hbm, qk_ref),
                (qv_hbm, qv_ref),
            ]
        )
    ]
    for copy in copies + passed:
        copy.start()
    rec_ref[...] = jnp.zeros_like(rec_ref)
    first_block = block_index() == 0
    qt_copy, k_copy, v_copy, qk_copy, qv_copy = copies
    for copy in (qt_copy, qk_copy, qv_copy):
        copy.wait()
    heads = qt_ref.shape[1] // HEAD_SIZE
    chunk = half // (heads * QUERY_TOKENS)
    for h in range(heads):
        q_ref[h * QUERY_TOKENS : (h + 1) * QUERY_TOKENS, :] = qt_ref[
            :, h * HEAD_SIZE : (h + 1) * HEAD_SIZE
        ].astype(F32)
    group = QUERY_PER_KEY * QUERY_TOKENS
    token = lax.broadcasted_iota(jnp.int32, (group, 1), 0) % QUERY_TOKENS
    groups = range(heads // QUERY_PER_KEY)
    cols = [slice(kv * HEAD_SIZE, (kv + 1) * HEAD_SIZE) for kv in groups]
    queries = [q_ref[kv * group : (kv + 1) * group, :] for kv in groups]
    own = []
    for kv in groups:
        new_k = qk_ref[:, cols[kv]].astype(F32)
        own.append([])
        for j in range(QUERY_TOKENS):
            s = jnp.sum(queries[kv] * new_k[j : j + 1, :], axis=-1, keepdims=True) * SCALE
            own[kv].append(jnp.where(jnp.logical_and(token >= j, first_block), s, NEG))
    k_copy.wait()
    scores = [dot_nt(queries[kv].astype(BF16), k_ref[:, cols[kv]]) * SCALE for kv in groups]
    tops = []
    for kv in groups:
        top = jnp.max(scores[kv], axis=-1, keepdims=True)
        for s in own[kv]:
            top = jnp.maximum(top, s)
        tops.append(top)
    expo = [jnp.exp(scores[kv] - tops[kv]) for kv in groups]
    v_copy.wait()
    mixes = [
        jnp.dot(expo[kv].astype(BF16), v_ref[:, cols[kv]], preferred_element_type=F32)
        for kv in groups
    ]
    full = (group, HEAD_SIZE)
    for kv in groups:
        new_v = qv_ref[:, cols[kv]].astype(F32)
        total = jnp.sum(expo[kv], axis=-1, keepdims=True)
        mixed = mixes[kv]
        for j, s in enumerate(own[kv]):
            e = jnp.exp(s - tops[kv])
            total = total + e
            mixed = mixed + e.astype(BF16).astype(F32) * new_v[j : j + 1, :]
        for k, value in enumerate(
            record_rows(jnp.broadcast_to(tops[kv], full), jnp.broadcast_to(total, full), mixed)
        ):
            rec_ref[pl.ds(kv * group * chunk + k, group, stride=chunk), :] = value
    out_ref[:, 2 * width :] = rec_ref[...].astype(BF16)
    for copy in passed:
        copy.wait()


def local_parts(inputs):
    rows, width = inputs[3].shape
    half = rows // 2
    hbm = pl.BlockSpec(memory_space=pltpu.HBM)
    return pl.pallas_call(
        local_kernel,
        out_shape=jax.ShapeDtypeStruct((half, 2 * width + HEAD_SIZE), BF16),
        in_specs=[hbm] * len(inputs),
        out_specs=pl.BlockSpec(memory_space=pltpu.VMEM),
        scratch_shapes=[pltpu.VMEM(array.shape, BF16) for array in inputs]
        + [
            pltpu.VMEM((half, HEAD_SIZE), F32),
            pltpu.VMEM((inputs[0].shape[1] // HEAD_SIZE * QUERY_TOKENS, HEAD_SIZE), F32),
            pltpu.SemaphoreType.DMA((7,)),
        ],
        compiler_params=pltpu.CompilerParams(vmem_limit_bytes=VMEM_LIMIT),
        name="local_parts",
    )(*(pltpu.with_memory_space_constraint(array, pltpu.HBM) for array in inputs))


def passing_on(send, moved, helpers):
    rows, width = moved.shape
    half = rows // 2

    def kernel(send_ref, moved_ref, out_ref):
        position = block_index() * 2 + lax.axis_index("tp")

        @pl.when(jnp.logical_or(position == helpers[0], position == helpers[1]))
        def _():
            for n in range(2):
                out_ref[:, n * width : (n + 1) * width] = moved_ref[n * half : (n + 1) * half, :]

    vmem = pl.BlockSpec(memory_space=pltpu.VMEM)
    return pl.pallas_call(
        kernel,
        out_shape=jax.ShapeDtypeStruct(send.shape, BF16),
        in_specs=[vmem] * 2,
        out_specs=vmem,
        input_output_aliases={0: 0},
        compiler_params=pltpu.CompilerParams(vmem_limit_bytes=VMEM_LIMIT),
        name="passing_on",
    )(send, moved)


def middle_kernel(chunk, rec_in_ref, piece_ref, out_ref, in_ref, rec_ref):
    last = piece_ref.shape[0] == chunk
    in_ref[...] = rec_in_ref[...].astype(F32)
    peak, total, mixed = merge_records(in_ref, in_ref.shape[0] // chunk, chunk)
    if last:
        rec_ref[...] = jnp.broadcast_to(mixed / total, rec_ref.shape)
    else:
        rec_ref[...] = jnp.zeros_like(rec_ref)
        for k, value in enumerate(record_rows(peak, total, mixed)):
            rec_ref[k : k + 1, :] = value
    record = rec_ref[...].astype(BF16)
    width = piece_ref.shape[1]
    for n in range(piece_ref.shape[0] // chunk):
        piece = piece_ref[n * chunk : (n + 1) * chunk, :]
        for at in range(0, out_ref.shape[0], chunk):
            out_ref[at : at + chunk, n * width : (n + 1) * width] = piece
    for at in range(0, out_ref.shape[0], chunk):
        out_ref[at : at + chunk, out_ref.shape[1] - HEAD_SIZE :] = record


def middle(received, chunk, copies, last):
    def kernel(*refs):
        middle_kernel(chunk, *refs)

    rows, total = received.shape
    width = total - HEAD_SIZE
    sources = 1 if last else 2
    shape = (copies * chunk, sources * width + HEAD_SIZE)
    return pl.pallas_call(
        kernel,
        grid=(1,),
        out_shape=jax.ShapeDtypeStruct(shape, BF16),
        in_specs=[
            pl.BlockSpec((rows, HEAD_SIZE), lambda i: (0, width // HEAD_SIZE)),
            pl.BlockSpec((sources * chunk, width), lambda i: (0, 0)),
        ],
        out_specs=pl.BlockSpec(shape, lambda i: (0, 0)),
        scratch_shapes=[
            pltpu.VMEM((rows, HEAD_SIZE), F32),
            pltpu.VMEM((chunk, HEAD_SIZE), F32),
        ],
        compiler_params=pltpu.CompilerParams(vmem_limit_bytes=VMEM_LIMIT),
        name="merge_last" if last else "merge_first",
    )(received, received)


def answer_kernel(rec_in_ref, out_ref, in_ref):
    heads = out_ref.shape[1] // HEAD_SIZE
    count = heads * QUERY_TOKENS
    in_ref[...] = rec_in_ref[...].astype(F32)
    found = in_ref[pl.ds(0, count, stride=in_ref.shape[0] // count), :]
    for h in range(heads):
        out_ref[:, h * HEAD_SIZE : (h + 1) * HEAD_SIZE] = found[
            h * QUERY_TOKENS : (h + 1) * QUERY_TOKENS
        ].astype(BF16)


def answer_rows(received, width):
    rows, total = received.shape
    shape = (QUERY_TOKENS, width)
    return pl.pallas_call(
        answer_kernel,
        grid=(1,),
        out_shape=jax.ShapeDtypeStruct(shape, BF16),
        in_specs=[pl.BlockSpec((rows, HEAD_SIZE), lambda i: (0, total // HEAD_SIZE - 1))],
        out_specs=pl.BlockSpec(shape, lambda i: (0, 0)),
        scratch_shapes=[pltpu.VMEM((rows, HEAD_SIZE), F32)],
        compiler_params=pltpu.CompilerParams(vmem_limit_bytes=VMEM_LIMIT),
        name="answer_rows",
    )(received)


def lanes(value):
    return jnp.broadcast_to(value, (value.shape[0], HEAD_SIZE))


def top_of(pieces):
    high = pieces[0]
    for piece in pieces[1:]:
        high = jnp.maximum(high, piece)
    return lanes(jnp.max(high, axis=-1, keepdims=True))


def split(scores):
    return [scores[:, c : c + HEAD_SIZE] for c in range(0, scores.shape[1], HEAD_SIZE)]


def exps(pieces, base):
    return jnp.concatenate([jnp.exp2(p * FACTOR - base).astype(BF16) for p in pieces], axis=1)


def with_ones(values):
    return jnp.concatenate([values, jnp.ones_like(values)], axis=1)


STEP = 256


def attend_heads(which, step, ahead, q_ref, kv_ref, k_ref, v_ref, out_hbm, out_ref, sems):
    rows = q_ref.shape[0]
    heads = q_ref.shape[1] // HEAD_SIZE
    heads_kv = heads // QUERY_PER_KEY
    off = jnp.where(block_index() > 0, 0.0, -NEG).astype(F32)
    line = lax.broadcasted_iota(jnp.int32, (step, step), 0)
    column = lax.broadcasted_iota(jnp.int32, (step, step), 1)
    keep = column <= line
    head = lambda n: slice(n * HEAD_SIZE, (n + 1) * HEAD_SIZE)
    far_values = [with_ones(kv_ref[:, head(2 * heads_kv + n)]) for n in range(2 * heads_kv)]
    values = [with_ones(v_ref[:, head(n)]) for n in range(heads_kv)]
    items = [(h, at) for h in which for at in range(0, rows, step)]
    copies = []

    def scores_of(h, at):
        kv = h // QUERY_PER_KEY
        q = q_ref[at : at + step, head(h)]
        return (
            dot_nt(q, kv_ref[:, head(kv)]),
            dot_nt(q, kv_ref[:, head(heads_kv + kv)]),
            dot_nt(q, k_ref[: at + step, head(kv)]),
        )

    coming = [scores_of(*item) for item in items[:ahead]]
    for n, (h, at) in enumerate(items):
        if n + ahead < len(items):
            coming.append(scores_of(*items[n + ahead]))
        far_0, far_1, near = coming.pop(0)
        kv = h // QUERY_PER_KEY
        end = at + step
        far = [split(far_0), split(far_1)]
        own = split(near[:, :at]) if at else []
        own += split(jnp.where(keep, near[:, at:], NEG))
        peak = jnp.maximum(top_of(far[0] + far[1]) - off, top_of(own))
        base = peak * FACTOR
        both = jnp.dot(exps(own, base), values[kv][:end], preferred_element_type=F32)
        for side in range(2):
            both += jnp.dot(
                exps(far[side], base + off),
                far_values[side * heads_kv + kv],
                preferred_element_type=F32,
            )
        out_ref[at:end, head(h)] = (both[:, :HEAD_SIZE] * (1.0 / both[:, HEAD_SIZE:])).astype(BF16)
        copy = pltpu.make_async_copy(
            out_ref.at[at:end, head(h)], out_hbm.at[at:end, head(h)], sems.at[n]
        )
        copy.start()
        copies.append(copy)
    for copy in copies:
        copy.wait()


def attend_early(document_query, received, document_key, document_value, answer_half):
    local = (document_query, document_key, document_value)
    shape = document_query.shape
    half = shape[1] // HEAD_SIZE // 2
    vmem = pl.BlockSpec(memory_space=pltpu.VMEM)
    hbm = pl.BlockSpec(memory_space=pltpu.HBM)

    def kernel(*refs):
        sources, kv_ref, rows_ref, out_hbm, rows_out_ref = refs[:3], *refs[3:7]
        targets, out_ref, sems, in_sems = refs[7:10], *refs[10:]
        rows_out_ref[...] = rows_ref[...]

        @pl.when(lax.axis_index("tp") == 1)
        def _():
            copies = [
                pltpu.make_async_copy(source, target, in_sems.at[n])
                for n, (source, target) in enumerate(zip(sources, targets))
            ]
            for copy in copies:
                copy.start()
            for copy in copies:
                copy.wait()
            q_ref, k_ref, v_ref = targets
            attend_heads(
                range(half), STEP, 1, q_ref, kv_ref, k_ref, v_ref, out_hbm, out_ref, sems
            )

    return pl.pallas_call(
        kernel,
        out_shape=(
            jax.ShapeDtypeStruct(shape, BF16),
            jax.ShapeDtypeStruct(answer_half.shape, BF16),
        ),
        in_specs=[hbm] * 3 + [vmem] * 2,
        out_specs=(hbm, vmem),
        scratch_shapes=[pltpu.VMEM(array.shape, BF16) for array in local]
        + [
            pltpu.VMEM(shape, BF16),
            pltpu.SemaphoreType.DMA((half * shape[0] // STEP,)),
            pltpu.SemaphoreType.DMA((3,)),
        ],
        compiler_params=pltpu.CompilerParams(vmem_limit_bytes=VMEM_LIMIT),
        name="attend_early",
    )(
        *(pltpu.with_memory_space_constraint(array, pltpu.HBM) for array in local),
        received,
        answer_half,
    )


def attend_late(document_query, received, document_key, document_value, ctx_out):
    shape = document_query.shape
    heads = shape[1] // HEAD_SIZE
    vmem = pl.BlockSpec(memory_space=pltpu.VMEM)
    hbm = pl.BlockSpec(memory_space=pltpu.HBM)

    def kernel(q_ref, kv_ref, k_ref, v_ref, _, out_hbm, out_ref, sems):
        refs = (q_ref, kv_ref, k_ref, v_ref, out_hbm, out_ref, sems)

        @pl.when(lax.axis_index("tp") == 0)
        def _():
            attend_heads(range(heads), STEP, 1, *refs)

        @pl.when(lax.axis_index("tp") == 1)
        def _():
            attend_heads(range(heads // 2, heads), STEP, 1, *refs)

    return pl.pallas_call(
        kernel,
        out_shape=jax.ShapeDtypeStruct(shape, BF16),
        in_specs=[vmem] * 4 + [hbm],
        out_specs=hbm,
        input_output_aliases={4: 0},
        scratch_shapes=[
            pltpu.VMEM(shape, BF16),
            pltpu.SemaphoreType.DMA((heads * shape[0] // STEP,)),
        ],
        compiler_params=pltpu.CompilerParams(vmem_limit_bytes=VMEM_LIMIT),
        name="attend_late",
    )(document_query, received, document_key, document_value, ctx_out)


def body(
    document_query,
    document_key,
    document_value,
    query_token_query,
    query_token_key,
    query_token_value,
):
    rows, width = document_key.shape
    planes, lines, root_planes = exchange_groups()
    peers = len(planes[0])
    chunk = rows // 2 // peers
    helpers = [plane[1] for plane in root_planes]
    moved = lax.ppermute(document_value, AXES, [tuple(plane[:2]) for plane in root_planes])
    inputs = (
        query_token_query,
        query_token_key,
        query_token_value,
        document_key,
        document_value,
    )
    send = passing_on(local_parts(inputs), moved, helpers)
    received = exchange(send, planes)
    send = middle(received, chunk, len(lines[0]), False)
    received = exchange(send, lines)
    send = middle(received, chunk, peers, True)
    received = exchange(send, planes)
    answer_half = answer_rows(received, query_token_query.shape[1])
    inputs = (document_query, received, document_key, document_value)
    ctx_out, sent_half = attend_early(*inputs, answer_half)
    other_half = lax.ppermute(sent_half, "tp", [(0, 1), (1, 0)])
    ctx_out = attend_late(*inputs, ctx_out)
    first = lax.axis_index("tp") == 0
    halves = (
        jnp.where(first, answer_half, other_half),
        jnp.where(first, other_half, answer_half),
    )
    return (ctx_out, jnp.concatenate(halves, axis=1))


def solution(mesh):
    grid = Mesh(mesh.devices.reshape(SIZES + (-1,)), ("y", "x", "z", "tp"))
    blk = ("y", "x", "z")
    placed = (P(blk, "tp"),) * 3 + (P(None, "tp"),) * 3
    return jax.shard_map(
        body, mesh=grid, in_specs=placed, out_specs=(P(blk, "tp"), P()), check_vma=False
    )
```

```python
import math

import jax
import jax.numpy as jnp
import numpy as np
from jax import lax
from jax.experimental import pallas as pl
from jax.experimental.pallas import tpu as pltpu
from jax.sharding import Mesh, PartitionSpec as P

HEAD_SIZE = 128
QUERY_PER_KEY = 4
QUERY_TOKENS = 4
SIZES = (8, 4, 8)
NEG = -1e30
F32 = jnp.float32
BF16 = jnp.bfloat16
SCALE = HEAD_SIZE**-0.5
LOG2E = math.log2(math.e)
VMEM_LIMIT = 40 * 1024 * 1024


FACTOR = SCALE * LOG2E


AXES = ("y", "x", "z", "tp")


def exchange_groups():
    ids = np.arange(2 * math.prod(SIZES)).reshape(SIZES + (2,))
    y, x, z = SIZES
    first = ids[..., 0].reshape(y * x, z)
    second = np.moveaxis(ids[..., 1], 0, -1).reshape(x * z, y)
    planes = np.concatenate([first.T, second.T]).tolist()
    lines = np.concatenate([first, second]).tolist()
    return planes, lines, (planes[0], planes[z])


def exchange(array, groups):
    return lax.all_to_all(array, AXES, 0, 0, tiled=True, axis_index_groups=groups)


def dot_nt(a, b):
    return lax.dot_general(a, b, (((1,), (1,)), ((), ())), preferred_element_type=F32)


def block_index():
    return (lax.axis_index("y") * SIZES[1] + lax.axis_index("x")) * SIZES[2] + lax.axis_index("z")


def parts_of(value, count):
    terms = []
    for _ in range(count - 1):
        term = value.astype(BF16).astype(F32)
        terms.append(term)
        value = value - term
    return terms + [value]


def record_rows(peak, total, mixed):
    return parts_of(mixed, 2) + parts_of(peak, 3) + parts_of(total, 2)


def merge_records(ref, count, stride):
    row = lambda k: ref[pl.ds(k, count, stride=stride), :]
    mixed = row(0) + row(1)
    peak = (row(2) + row(3)) + row(4)
    total = row(5) + row(6)
    top = jnp.max(peak, axis=0, keepdims=True)
    weight = jnp.exp(peak - top)
    return (
        top,
        jnp.sum(total * weight, axis=0, keepdims=True),
        jnp.sum(mixed * weight, axis=0, keepdims=True),
    )


def local_kernel(
    qt_hbm,
    qk_hbm,
    qv_hbm,
    k_hbm,
    v_hbm,
    out_ref,
    qt_ref,
    qk_ref,
    qv_ref,
    k_ref,
    v_ref,
    rec_ref,
    q_ref,
    sems,
):
    rows, width = k_hbm.shape
    half = rows // 2
    passed = [
        pltpu.make_async_copy(
            k_hbm.at[n * half : (n + 1) * half, :],
            out_ref.at[:, n * width : (n + 1) * width],
            sems.at[n],
        )
        for n in range(2)
    ]
    copies = [
        pltpu.make_async_copy(source, target, sems.at[2 + n])
        for n, (source, target) in enumerate(
            [
                (qt_hbm, qt_ref),
                (k_hbm, k_ref),
                (v_hbm, v_ref),
                (qk_hbm, qk_ref),
                (qv_hbm, qv_ref),
            ]
        )
    ]
    for copy in copies + passed:
        copy.start()
    rec_ref[...] = jnp.zeros_like(rec_ref)
    first_block = block_index() == 0
    qt_copy, k_copy, v_copy, qk_copy, qv_copy = copies
    for copy in (qt_copy, qk_copy, qv_copy):
        copy.wait()
    heads = qt_ref.shape[1] // HEAD_SIZE
    chunk = half // (heads * QUERY_TOKENS)
    for h in range(heads):
        q_ref[h * QUERY_TOKENS : (h + 1) * QUERY_TOKENS, :] = qt_ref[
            :, h * HEAD_SIZE : (h + 1) * HEAD_SIZE
        ].astype(F32)
    group = QUERY_PER_KEY * QUERY_TOKENS
    token = lax.broadcasted_iota(jnp.int32, (group, 1), 0) % QUERY_TOKENS
    groups = range(heads // QUERY_PER_KEY)
    cols = [slice(kv * HEAD_SIZE, (kv + 1) * HEAD_SIZE) for kv in groups]
    queries = [q_ref[kv * group : (kv + 1) * group, :] for kv in groups]
    own = []
    for kv in groups:
        new_k = qk_ref[:, cols[kv]].astype(F32)
        own.append([])
        for j in range(QUERY_TOKENS):
            s = jnp.sum(queries[kv] * new_k[j : j + 1, :], axis=-1, keepdims=True) * SCALE
            own[kv].append(jnp.where(jnp.logical_and(token >= j, first_block), s, NEG))
    k_copy.wait()
    scores = [dot_nt(queries[kv].astype(BF16), k_ref[:, cols[kv]]) * SCALE for kv in groups]
    tops = []
    for kv in groups:
        top = jnp.max(scores[kv], axis=-1, keepdims=True)
        for s in own[kv]:
            top = jnp.maximum(top, s)
        tops.append(top)
    expo = [jnp.exp(scores[kv] - tops[kv]) for kv in groups]
    v_copy.wait()
    mixes = [
        jnp.dot(expo[kv].astype(BF16), v_ref[:, cols[kv]], preferred_element_type=F32)
        for kv in groups
    ]
    full = (group, HEAD_SIZE)
    for kv in groups:
        new_v = qv_ref[:, cols[kv]].astype(F32)
        total = jnp.sum(expo[kv], axis=-1, keepdims=True)
        mixed = mixes[kv]
        for j, s in enumerate(own[kv]):
            e = jnp.exp(s - tops[kv])
            total = total + e
            mixed = mixed + e.astype(BF16).astype(F32) * new_v[j : j + 1, :]
        for k, value in enumerate(
            record_rows(jnp.broadcast_to(tops[kv], full), jnp.broadcast_to(total, full), mixed)
        ):
            rec_ref[pl.ds(kv * group * chunk + k, group, stride=chunk), :] = value
    out_ref[:, 2 * width :] = rec_ref[...].astype(BF16)
    for copy in passed:
        copy.wait()


def local_parts(inputs):
    rows, width = inputs[3].shape
    half = rows // 2
    hbm = pl.BlockSpec(memory_space=pltpu.HBM)
    return pl.pallas_call(
        local_kernel,
        out_shape=jax.ShapeDtypeStruct((half, 2 * width + HEAD_SIZE), BF16),
        in_specs=[hbm] * len(inputs),
        out_specs=pl.BlockSpec(memory_space=pltpu.VMEM),
        scratch_shapes=[pltpu.VMEM(array.shape, BF16) for array in inputs]
        + [
            pltpu.VMEM((half, HEAD_SIZE), F32),
            pltpu.VMEM((inputs[0].shape[1] // HEAD_SIZE * QUERY_TOKENS, HEAD_SIZE), F32),
            pltpu.SemaphoreType.DMA((7,)),
        ],
        compiler_params=pltpu.CompilerParams(vmem_limit_bytes=VMEM_LIMIT),
        name="local_parts",
    )(*(pltpu.with_memory_space_constraint(array, pltpu.HBM) for array in inputs))


def passing_on(send, moved, helpers):
    rows, width = moved.shape
    half = rows // 2

    def kernel(send_ref, moved_ref, out_ref):
        position = block_index() * 2 + lax.axis_index("tp")

        @pl.when(jnp.logical_or(position == helpers[0], position == helpers[1]))
        def _():
            for n in range(2):
                out_ref[:, n * width : (n + 1) * width] = moved_ref[n * half : (n + 1) * half, :]

    vmem = pl.BlockSpec(memory_space=pltpu.VMEM)
    return pl.pallas_call(
        kernel,
        out_shape=jax.ShapeDtypeStruct(send.shape, BF16),
        in_specs=[vmem] * 2,
        out_specs=vmem,
        input_output_aliases={0: 0},
        compiler_params=pltpu.CompilerParams(vmem_limit_bytes=VMEM_LIMIT),
        name="passing_on",
    )(send, moved)


def middle_kernel(chunk, rec_in_ref, piece_ref, out_ref, in_ref, rec_ref):
    last = piece_ref.shape[0] == chunk
    in_ref[...] = rec_in_ref[...].astype(F32)
    peak, total, mixed = merge_records(in_ref, in_ref.shape[0] // chunk, chunk)
    if last:
        rec_ref[...] = jnp.broadcast_to(mixed / total, rec_ref.shape)
    else:
        rec_ref[...] = jnp.zeros_like(rec_ref)
        for k, value in enumerate(record_rows(peak, total, mixed)):
            rec_ref[k : k + 1, :] = value
    record = rec_ref[...].astype(BF16)
    width = piece_ref.shape[1]
    for n in range(piece_ref.shape[0] // chunk):
        piece = piece_ref[n * chunk : (n + 1) * chunk, :]
        for at in range(0, out_ref.shape[0], chunk):
            out_ref[at : at + chunk, n * width : (n + 1) * width] = piece
    for at in range(0, out_ref.shape[0], chunk):
        out_ref[at : at + chunk, out_ref.shape[1] - HEAD_SIZE :] = record


def middle(received, chunk, copies, last):
    def kernel(*refs):
        middle_kernel(chunk, *refs)

    rows, total = received.shape
    width = total - HEAD_SIZE
    sources = 1 if last else 2
    shape = (copies * chunk, sources * width + HEAD_SIZE)
    return pl.pallas_call(
        kernel,
        grid=(1,),
        out_shape=jax.ShapeDtypeStruct(shape, BF16),
        in_specs=[
            pl.BlockSpec((rows, HEAD_SIZE), lambda i: (0, width // HEAD_SIZE)),
            pl.BlockSpec((sources * chunk, width), lambda i: (0, 0)),
        ],
        out_specs=pl.BlockSpec(shape, lambda i: (0, 0)),
        scratch_shapes=[
            pltpu.VMEM((rows, HEAD_SIZE), F32),
            pltpu.VMEM((chunk, HEAD_SIZE), F32),
        ],
        compiler_params=pltpu.CompilerParams(vmem_limit_bytes=VMEM_LIMIT),
        name="merge_last" if last else "merge_first",
    )(received, received)


def answer_kernel(rec_in_ref, out_ref, in_ref):
    heads = out_ref.shape[1] // HEAD_SIZE
    count = heads * QUERY_TOKENS
    in_ref[...] = rec_in_ref[...].astype(F32)
    found = in_ref[pl.ds(0, count, stride=in_ref.shape[0] // count), :]
    for h in range(heads):
        out_ref[:, h * HEAD_SIZE : (h + 1) * HEAD_SIZE] = found[
            h * QUERY_TOKENS : (h + 1) * QUERY_TOKENS
        ].astype(BF16)


def answer_rows(received, width):
    rows, total = received.shape
    shape = (QUERY_TOKENS, width)
    return pl.pallas_call(
        answer_kernel,
        grid=(1,),
        out_shape=jax.ShapeDtypeStruct(shape, BF16),
        in_specs=[pl.BlockSpec((rows, HEAD_SIZE), lambda i: (0, total // HEAD_SIZE - 1))],
        out_specs=pl.BlockSpec(shape, lambda i: (0, 0)),
        scratch_shapes=[pltpu.VMEM((rows, HEAD_SIZE), F32)],
        compiler_params=pltpu.CompilerParams(vmem_limit_bytes=VMEM_LIMIT),
        name="answer_rows",
    )(received)


def lanes(value):
    return jnp.broadcast_to(value, (value.shape[0], HEAD_SIZE))


def top_of(pieces):
    high = pieces[0]
    for piece in pieces[1:]:
        high = jnp.maximum(high, piece)
    return lanes(jnp.max(high, axis=-1, keepdims=True))


def split(scores):
    return [scores[:, c : c + HEAD_SIZE] for c in range(0, scores.shape[1], HEAD_SIZE)]


def exps(pieces, base):
    return jnp.concatenate([jnp.exp2(p * FACTOR - base).astype(BF16) for p in pieces], axis=1)


def with_ones(values):
    return jnp.concatenate([values, jnp.ones_like(values)], axis=1)


STEP = 256


def attend_heads(which, step, ahead, q_ref, kv_ref, k_ref, v_ref, out_hbm, out_ref, sems):
    rows = q_ref.shape[0]
    heads = q_ref.shape[1] // HEAD_SIZE
    heads_kv = heads // QUERY_PER_KEY
    off = jnp.where(block_index() > 0, 0.0, -NEG).astype(F32)
    line = lax.broadcasted_iota(jnp.int32, (step, step), 0)
    column = lax.broadcasted_iota(jnp.int32, (step, step), 1)
    keep = column <= line
    head = lambda n: slice(n * HEAD_SIZE, (n + 1) * HEAD_SIZE)
    far_values = [with_ones(kv_ref[:, head(2 * heads_kv + n)]) for n in range(2 * heads_kv)]
    values = [with_ones(v_ref[:, head(n)]) for n in range(heads_kv)]
    items = [(h, at) for h in which for at in range(0, rows, step)]
    copies = []

    def scores_of(h, at):
        kv = h // QUERY_PER_KEY
        q = q_ref[at : at + step, head(h)]
        return (
            dot_nt(q, kv_ref[:, head(kv)]),
            dot_nt(q, kv_ref[:, head(heads_kv + kv)]),
            dot_nt(q, k_ref[: at + step, head(kv)]),
        )

    coming = [scores_of(*item) for item in items[:ahead]]
    for n, (h, at) in enumerate(items):
        if n + ahead < len(items):
            coming.append(scores_of(*items[n + ahead]))
        far_0, far_1, near = coming.pop(0)
        kv = h // QUERY_PER_KEY
        end = at + step
        far = [split(far_0), split(far_1)]
        own = split(near[:, :at]) if at else []
        own += split(jnp.where(keep, near[:, at:], NEG))
        peak = jnp.maximum(top_of(far[0] + far[1]) - off, top_of(own))
        base = peak * FACTOR
        both = jnp.dot(exps(own, base), values[kv][:end], preferred_element_type=F32)
        for side in range(2):
            both += jnp.dot(
                exps(far[side], base + off),
                far_values[side * heads_kv + kv],
                preferred_element_type=F32,
            )
        out_ref[at:end, head(h)] = (both[:, :HEAD_SIZE] * (1.0 / both[:, HEAD_SIZE:])).astype(BF16)
        copy = pltpu.make_async_copy(
            out_ref.at[at:end, head(h)], out_hbm.at[at:end, head(h)], sems.at[n]
        )
        copy.start()
        copies.append(copy)
    for copy in copies:
        copy.wait()


def attend_early(document_query, received, document_key, document_value, answer_half):
    local = (document_query, document_key, document_value)
    shape = document_query.shape
    half = shape[1] // HEAD_SIZE // 2
    vmem = pl.BlockSpec(memory_space=pltpu.VMEM)
    hbm = pl.BlockSpec(memory_space=pltpu.HBM)

    def kernel(*refs):
        sources, kv_ref, rows_ref, out_hbm, rows_out_ref = refs[:3], *refs[3:7]
        targets, out_ref, sems, in_sems = refs[7:10], *refs[10:]
        rows_out_ref[...] = rows_ref[...]

        @pl.when(lax.axis_index("tp") == 1)
        def _():
            copies = [
                pltpu.make_async_copy(
                    source.at[:, : source.shape[1] // 2],
                    target.at[:, : source.shape[1] // 2],
                    in_sems.at[n],
                )
                for n, (source, target) in enumerate(zip(sources, targets))
            ]
            for copy in copies:
                copy.start()
            for copy in copies:
                copy.wait()
            q_ref, k_ref, v_ref = targets
            attend_heads(
                range(half), STEP, 1, q_ref, kv_ref, k_ref, v_ref, out_hbm, out_ref, sems
            )

    return pl.pallas_call(
        kernel,
        out_shape=(
            jax.ShapeDtypeStruct(shape, BF16),
            jax.ShapeDtypeStruct(answer_half.shape, BF16),
        ),
        in_specs=[hbm] * 3 + [vmem] * 2,
        out_specs=(hbm, vmem),
        scratch_shapes=[pltpu.VMEM(array.shape, BF16) for array in local]
        + [
            pltpu.VMEM(shape, BF16),
            pltpu.SemaphoreType.DMA((half * shape[0] // STEP,)),
            pltpu.SemaphoreType.DMA((3,)),
        ],
        compiler_params=pltpu.CompilerParams(vmem_limit_bytes=VMEM_LIMIT),
        name="attend_early",
    )(
        *(pltpu.with_memory_space_constraint(array, pltpu.HBM) for array in local),
        received,
        answer_half,
    )


def attend_late(document_query, received, document_key, document_value, ctx_out):
    shape = document_query.shape
    heads = shape[1] // HEAD_SIZE
    vmem = pl.BlockSpec(memory_space=pltpu.VMEM)
    hbm = pl.BlockSpec(memory_space=pltpu.HBM)

    def kernel(q_ref, kv_ref, k_ref, v_ref, _, out_hbm, out_ref, sems):
        refs = (q_ref, kv_ref, k_ref, v_ref, out_hbm, out_ref, sems)

        @pl.when(lax.axis_index("tp") == 0)
        def _():
            attend_heads(range(heads), STEP, 1, *refs)

        @pl.when(lax.axis_index("tp") == 1)
        def _():
            attend_heads(range(heads // 2, heads), STEP, 1, *refs)

    return pl.pallas_call(
        kernel,
        out_shape=jax.ShapeDtypeStruct(shape, BF16),
        in_specs=[vmem] * 4 + [hbm],
        out_specs=hbm,
        input_output_aliases={4: 0},
        scratch_shapes=[
            pltpu.VMEM(shape, BF16),
            pltpu.SemaphoreType.DMA((heads * shape[0] // STEP,)),
        ],
        compiler_params=pltpu.CompilerParams(vmem_limit_bytes=VMEM_LIMIT),
        name="attend_late",
    )(document_query, received, document_key, document_value, ctx_out)


def body(
    document_query,
    document_key,
    document_value,
    query_token_query,
    query_token_key,
    query_token_value,
):
    rows, width = document_key.shape
    planes, lines, root_planes = exchange_groups()
    peers = len(planes[0])
    chunk = rows // 2 // peers
    helpers = [plane[1] for plane in root_planes]
    moved = lax.ppermute(document_value, AXES, [tuple(plane[:2]) for plane in root_planes])
    inputs = (
        query_token_query,
        query_token_key,
        query_token_value,
        document_key,
        document_value,
    )
    send = passing_on(local_parts(inputs), moved, helpers)
    received = exchange(send, planes)
    send = middle(received, chunk, len(lines[0]), False)
    received = exchange(send, lines)
    send = middle(received, chunk, peers, True)
    received = exchange(send, planes)
    answer_half = answer_rows(received, query_token_query.shape[1])
    inputs = (document_query, received, document_key, document_value)
    ctx_out, sent_half = attend_early(*inputs, answer_half)
    other_half = lax.ppermute(sent_half, "tp", [(0, 1), (1, 0)])
    ctx_out = attend_late(*inputs, ctx_out)
    first = lax.axis_index("tp") == 0
    halves = (
        jnp.where(first, answer_half, other_half),
        jnp.where(first, other_half, answer_half),
    )
    return (ctx_out, jnp.concatenate(halves, axis=1))


def solution(mesh):
    grid = Mesh(mesh.devices.reshape(SIZES + (-1,)), ("y", "x", "z", "tp"))
    blk = ("y", "x", "z")
    placed = (P(blk, "tp"),) * 3 + (P(None, "tp"),) * 3
    return jax.shard_map(
        body, mesh=grid, in_specs=placed, out_specs=(P(blk, "tp"), P()), check_vma=False
    )
```

```python
import math

import jax
import jax.numpy as jnp
import numpy as np
from jax import lax
from jax.experimental import pallas as pl
from jax.experimental.pallas import tpu as pltpu
from jax.sharding import Mesh, PartitionSpec as P

HEAD_SIZE = 128
QUERY_PER_KEY = 4
QUERY_TOKENS = 4
SIZES = (8, 4, 8)
NEG = -1e30
F32 = jnp.float32
BF16 = jnp.bfloat16
SCALE = HEAD_SIZE**-0.5
LOG2E = math.log2(math.e)
VMEM_LIMIT = 40 * 1024 * 1024


FACTOR = SCALE * LOG2E


AXES = ("y", "x", "z", "tp")


def exchange_groups():
    ids = np.arange(2 * math.prod(SIZES)).reshape(SIZES + (2,))
    y, x, z = SIZES
    first = ids[..., 0].reshape(y * x, z)
    second = np.moveaxis(ids[..., 1], 0, -1).reshape(x * z, y)
    planes = np.concatenate([first.T, second.T]).tolist()
    lines = np.concatenate([first, second]).tolist()
    return planes, lines, (planes[0], planes[z])


def exchange(array, groups):
    return lax.all_to_all(array, AXES, 0, 0, tiled=True, axis_index_groups=groups)


def dot_nt(a, b):
    return lax.dot_general(a, b, (((1,), (1,)), ((), ())), preferred_element_type=F32)


def block_index():
    return (lax.axis_index("y") * SIZES[1] + lax.axis_index("x")) * SIZES[2] + lax.axis_index("z")


def parts_of(value, count):
    terms = []
    for _ in range(count - 1):
        term = value.astype(BF16).astype(F32)
        terms.append(term)
        value = value - term
    return terms + [value]


def record_rows(peak, total, mixed):
    return parts_of(mixed, 2) + parts_of(peak, 3) + parts_of(total, 2)


def merge_records(ref, count, stride):
    row = lambda k: ref[pl.ds(k, count, stride=stride), :]
    mixed = row(0) + row(1)
    peak = (row(2) + row(3)) + row(4)
    total = row(5) + row(6)
    top = jnp.max(peak, axis=0, keepdims=True)
    weight = jnp.exp(peak - top)
    return (
        top,
        jnp.sum(total * weight, axis=0, keepdims=True),
        jnp.sum(mixed * weight, axis=0, keepdims=True),
    )


def local_kernel(
    qt_hbm,
    qk_hbm,
    qv_hbm,
    k_hbm,
    v_hbm,
    out_ref,
    qt_ref,
    qk_ref,
    qv_ref,
    k_ref,
    v_ref,
    rec_ref,
    q_ref,
    sems,
):
    rows, width = k_hbm.shape
    half = rows // 2
    passed = [
        pltpu.make_async_copy(
            k_hbm.at[n * half : (n + 1) * half, :],
            out_ref.at[:, n * width : (n + 1) * width],
            sems.at[n],
        )
        for n in range(2)
    ]
    copies = [
        pltpu.make_async_copy(source, target, sems.at[2 + n])
        for n, (source, target) in enumerate(
            [
                (qt_hbm, qt_ref),
                (k_hbm, k_ref),
                (v_hbm, v_ref),
                (qk_hbm, qk_ref),
                (qv_hbm, qv_ref),
            ]
        )
    ]
    for copy in copies + passed:
        copy.start()
    rec_ref[...] = jnp.zeros_like(rec_ref)
    first_block = block_index() == 0
    qt_copy, k_copy, v_copy, qk_copy, qv_copy = copies
    for copy in (qt_copy, qk_copy, qv_copy):
        copy.wait()
    heads = qt_ref.shape[1] // HEAD_SIZE
    chunk = half // (heads * QUERY_TOKENS)
    for h in range(heads):
        q_ref[h * QUERY_TOKENS : (h + 1) * QUERY_TOKENS, :] = qt_ref[
            :, h * HEAD_SIZE : (h + 1) * HEAD_SIZE
        ].astype(F32)
    group = QUERY_PER_KEY * QUERY_TOKENS
    token = lax.broadcasted_iota(jnp.int32, (group, 1), 0) % QUERY_TOKENS
    groups = range(heads // QUERY_PER_KEY)
    cols = [slice(kv * HEAD_SIZE, (kv + 1) * HEAD_SIZE) for kv in groups]
    queries = [q_ref[kv * group : (kv + 1) * group, :] for kv in groups]
    own = []
    for kv in groups:
        new_k = qk_ref[:, cols[kv]].astype(F32)
        own.append([])
        for j in range(QUERY_TOKENS):
            s = jnp.sum(queries[kv] * new_k[j : j + 1, :], axis=-1, keepdims=True) * SCALE
            own[kv].append(jnp.where(jnp.logical_and(token >= j, first_block), s, NEG))
    k_copy.wait()
    scores = [dot_nt(queries[kv].astype(BF16), k_ref[:, cols[kv]]) * SCALE for kv in groups]
    tops = []
    for kv in groups:
        top = jnp.max(scores[kv], axis=-1, keepdims=True)
        for s in own[kv]:
            top = jnp.maximum(top, s)
        tops.append(top)
    expo = [jnp.exp(scores[kv] - tops[kv]) for kv in groups]
    v_copy.wait()
    mixes = [
        jnp.dot(expo[kv].astype(BF16), v_ref[:, cols[kv]], preferred_element_type=F32)
        for kv in groups
    ]
    full = (group, HEAD_SIZE)
    for kv in groups:
        new_v = qv_ref[:, cols[kv]].astype(F32)
        total = jnp.sum(expo[kv], axis=-1, keepdims=True)
        mixed = mixes[kv]
        for j, s in enumerate(own[kv]):
            e = jnp.exp(s - tops[kv])
            total = total + e
            mixed = mixed + e.astype(BF16).astype(F32) * new_v[j : j + 1, :]
        for k, value in enumerate(
            record_rows(jnp.broadcast_to(tops[kv], full), jnp.broadcast_to(total, full), mixed)
        ):
            rec_ref[pl.ds(kv * group * chunk + k, group, stride=chunk), :] = value
    out_ref[:, 2 * width :] = rec_ref[...].astype(BF16)
    for copy in passed:
        copy.wait()


def local_parts(inputs):
    rows, width = inputs[3].shape
    half = rows // 2
    hbm = pl.BlockSpec(memory_space=pltpu.HBM)
    return pl.pallas_call(
        local_kernel,
        out_shape=jax.ShapeDtypeStruct((half, 2 * width + HEAD_SIZE), BF16),
        in_specs=[hbm] * len(inputs),
        out_specs=pl.BlockSpec(memory_space=pltpu.VMEM),
        scratch_shapes=[pltpu.VMEM(array.shape, BF16) for array in inputs]
        + [
            pltpu.VMEM((half, HEAD_SIZE), F32),
            pltpu.VMEM((inputs[0].shape[1] // HEAD_SIZE * QUERY_TOKENS, HEAD_SIZE), F32),
            pltpu.SemaphoreType.DMA((7,)),
        ],
        compiler_params=pltpu.CompilerParams(vmem_limit_bytes=VMEM_LIMIT),
        name="local_parts",
    )(*(pltpu.with_memory_space_constraint(array, pltpu.HBM) for array in inputs))


def passing_on(send, moved, helpers):
    rows, width = moved.shape
    half = rows // 2

    def kernel(send_ref, moved_ref, out_ref):
        position = block_index() * 2 + lax.axis_index("tp")

        @pl.when(jnp.logical_or(position == helpers[0], position == helpers[1]))
        def _():
            for n in range(2):
                out_ref[:, n * width : (n + 1) * width] = moved_ref[n * half : (n + 1) * half, :]

    vmem = pl.BlockSpec(memory_space=pltpu.VMEM)
    return pl.pallas_call(
        kernel,
        out_shape=jax.ShapeDtypeStruct(send.shape, BF16),
        in_specs=[vmem] * 2,
        out_specs=vmem,
        input_output_aliases={0: 0},
        compiler_params=pltpu.CompilerParams(vmem_limit_bytes=VMEM_LIMIT),
        name="passing_on",
    )(send, moved)


def middle_kernel(chunk, rec_in_ref, piece_ref, out_ref, in_ref, rec_ref):
    last = piece_ref.shape[0] == chunk
    in_ref[...] = rec_in_ref[...].astype(F32)
    peak, total, mixed = merge_records(in_ref, in_ref.shape[0] // chunk, chunk)
    if last:
        rec_ref[...] = jnp.broadcast_to(mixed / total, rec_ref.shape)
    else:
        rec_ref[...] = jnp.zeros_like(rec_ref)
        for k, value in enumerate(record_rows(peak, total, mixed)):
            rec_ref[k : k + 1, :] = value
    record = rec_ref[...].astype(BF16)
    width = piece_ref.shape[1]
    for n in range(piece_ref.shape[0] // chunk):
        piece = piece_ref[n * chunk : (n + 1) * chunk, :]
        for at in range(0, out_ref.shape[0], chunk):
            out_ref[at : at + chunk, n * width : (n + 1) * width] = piece
    for at in range(0, out_ref.shape[0], chunk):
        out_ref[at : at + chunk, out_ref.shape[1] - HEAD_SIZE :] = record


def middle(received, chunk, copies, last):
    def kernel(*refs):
        middle_kernel(chunk, *refs)

    rows, total = received.shape
    width = total - HEAD_SIZE
    sources = 1 if last else 2
    shape = (copies * chunk, sources * width + HEAD_SIZE)
    return pl.pallas_call(
        kernel,
        grid=(1,),
        out_shape=jax.ShapeDtypeStruct(shape, BF16),
        in_specs=[
            pl.BlockSpec((rows, HEAD_SIZE), lambda i: (0, width // HEAD_SIZE)),
            pl.BlockSpec((sources * chunk, width), lambda i: (0, 0)),
        ],
        out_specs=pl.BlockSpec(shape, lambda i: (0, 0)),
        scratch_shapes=[
            pltpu.VMEM((rows, HEAD_SIZE), F32),
            pltpu.VMEM((chunk, HEAD_SIZE), F32),
        ],
        compiler_params=pltpu.CompilerParams(vmem_limit_bytes=VMEM_LIMIT),
        name="merge_last" if last else "merge_first",
    )(received, received)


def answer_kernel(rec_in_ref, out_ref, in_ref):
    heads = out_ref.shape[1] // HEAD_SIZE
    count = heads * QUERY_TOKENS
    in_ref[...] = rec_in_ref[...].astype(F32)
    found = in_ref[pl.ds(0, count, stride=in_ref.shape[0] // count), :]
    for h in range(heads):
        out_ref[:, h * HEAD_SIZE : (h + 1) * HEAD_SIZE] = found[
            h * QUERY_TOKENS : (h + 1) * QUERY_TOKENS
        ].astype(BF16)


def answer_rows(received, width):
    rows, total = received.shape
    shape = (QUERY_TOKENS, width)
    return pl.pallas_call(
        answer_kernel,
        grid=(1,),
        out_shape=jax.ShapeDtypeStruct(shape, BF16),
        in_specs=[pl.BlockSpec((rows, HEAD_SIZE), lambda i: (0, total // HEAD_SIZE - 1))],
        out_specs=pl.BlockSpec(shape, lambda i: (0, 0)),
        scratch_shapes=[pltpu.VMEM((rows, HEAD_SIZE), F32)],
        compiler_params=pltpu.CompilerParams(vmem_limit_bytes=VMEM_LIMIT),
        name="answer_rows",
    )(received)


def lanes(value):
    return jnp.broadcast_to(value, (value.shape[0], HEAD_SIZE))


def top_of(pieces):
    high = pieces[0]
    for piece in pieces[1:]:
        high = jnp.maximum(high, piece)
    return lanes(jnp.max(high, axis=-1, keepdims=True))


def split(scores):
    return [scores[:, c : c + HEAD_SIZE] for c in range(0, scores.shape[1], HEAD_SIZE)]


def exps(pieces, base):
    return jnp.concatenate([jnp.exp2(p * FACTOR - base).astype(BF16) for p in pieces], axis=1)


def with_ones(values):
    return jnp.concatenate([values, jnp.ones_like(values)], axis=1)


STEP = 256


def attend_heads(
    which, step, ahead, q_ref, kv_ref, k_ref, v_ref, out_hbm, out_ref, sems, loads=()
):
    rows = q_ref.shape[0]
    heads = q_ref.shape[1] // HEAD_SIZE
    heads_kv = heads // QUERY_PER_KEY
    off = jnp.where(block_index() > 0, 0.0, -NEG).astype(F32)
    line = lax.broadcasted_iota(jnp.int32, (step, step), 0)
    column = lax.broadcasted_iota(jnp.int32, (step, step), 1)
    keep = column <= line
    head = lambda n: slice(n * HEAD_SIZE, (n + 1) * HEAD_SIZE)
    far_values = [with_ones(kv_ref[:, head(2 * heads_kv + n)]) for n in range(2 * heads_kv)]
    values = [with_ones(v_ref[:, head(n)]) for n in range(heads_kv)]
    items = [(h, at) for h in which for at in range(0, rows, step)]
    copies = []

    def scores_of(h, at):
        kv = h // QUERY_PER_KEY
        if loads and at == 0:
            loads[h].wait()
        q = q_ref[at : at + step, head(h)]
        return (
            dot_nt(q, kv_ref[:, head(kv)]),
            dot_nt(q, kv_ref[:, head(heads_kv + kv)]),
            dot_nt(q, k_ref[: at + step, head(kv)]),
        )

    coming = [scores_of(*item) for item in items[:ahead]]
    for n, (h, at) in enumerate(items):
        if n + ahead < len(items):
            coming.append(scores_of(*items[n + ahead]))
        far_0, far_1, near = coming.pop(0)
        kv = h // QUERY_PER_KEY
        end = at + step
        far = [split(far_0), split(far_1)]
        own = split(near[:, :at]) if at else []
        own += split(jnp.where(keep, near[:, at:], NEG))
        peak = jnp.maximum(top_of(far[0] + far[1]) - off, top_of(own))
        base = peak * FACTOR
        both = jnp.dot(exps(own, base), values[kv][:end], preferred_element_type=F32)
        for side in range(2):
            both += jnp.dot(
                exps(far[side], base + off),
                far_values[side * heads_kv + kv],
                preferred_element_type=F32,
            )
        out_ref[at:end, head(h)] = (both[:, :HEAD_SIZE] * (1.0 / both[:, HEAD_SIZE:])).astype(BF16)
        copy = pltpu.make_async_copy(
            out_ref.at[at:end, head(h)], out_hbm.at[at:end, head(h)], sems.at[n]
        )
        copy.start()
        copies.append(copy)
    for copy in copies:
        copy.wait()


def attend_early(document_query, received, document_key, document_value, answer_half):
    local = (document_query, document_key, document_value)
    shape = document_query.shape
    half = shape[1] // HEAD_SIZE // 2
    vmem = pl.BlockSpec(memory_space=pltpu.VMEM)
    hbm = pl.BlockSpec(memory_space=pltpu.HBM)

    def kernel(*args):
        sources, kv_ref, rows_ref, out_hbm, rows_out_ref = args[:3], *args[3:7]
        targets, out_ref, sems, in_sems = args[7:10], *args[10:]
        rows_out_ref[...] = rows_ref[...]

        @pl.when(lax.axis_index("tp") == 1)
        def _():
            q_ref, k_ref, v_ref = targets
            pairs = [
                (source.at[:, : source.shape[1] // 2], target.at[:, : source.shape[1] // 2])
                for source, target in zip(sources[1:], targets[1:])
            ]
            for h in range(half):
                cols = slice(h * HEAD_SIZE, (h + 1) * HEAD_SIZE)
                pairs.append((sources[0].at[:, cols], q_ref.at[:, cols]))
            copies = [
                pltpu.make_async_copy(source, target, in_sems.at[n])
                for n, (source, target) in enumerate(pairs)
            ]
            for copy in copies:
                copy.start()
            for copy in copies[:2]:
                copy.wait()
            refs = (q_ref, kv_ref, k_ref, v_ref, out_hbm, out_ref, sems)
            attend_heads(range(half), STEP, 1, *refs, loads=copies[2:])

    return pl.pallas_call(
        kernel,
        out_shape=(
            jax.ShapeDtypeStruct(shape, BF16),
            jax.ShapeDtypeStruct(answer_half.shape, BF16),
        ),
        in_specs=[hbm] * 3 + [vmem] * 2,
        out_specs=(hbm, vmem),
        scratch_shapes=[pltpu.VMEM(array.shape, BF16) for array in local]
        + [
            pltpu.VMEM(shape, BF16),
            pltpu.SemaphoreType.DMA((half * shape[0] // STEP,)),
            pltpu.SemaphoreType.DMA((2 + half,)),
        ],
        compiler_params=pltpu.CompilerParams(vmem_limit_bytes=VMEM_LIMIT),
        name="attend_early",
    )(
        *(pltpu.with_memory_space_constraint(array, pltpu.HBM) for array in local),
        received,
        answer_half,
    )


def attend_late(document_query, received, document_key, document_value, ctx_out):
    shape = document_query.shape
    heads = shape[1] // HEAD_SIZE
    vmem = pl.BlockSpec(memory_space=pltpu.VMEM)
    hbm = pl.BlockSpec(memory_space=pltpu.HBM)

    def kernel(q_ref, kv_ref, k_ref, v_ref, _, out_hbm, out_ref, sems):
        refs = (q_ref, kv_ref, k_ref, v_ref, out_hbm, out_ref, sems)

        @pl.when(lax.axis_index("tp") == 0)
        def _():
            attend_heads(range(heads), STEP, 1, *refs)

        @pl.when(lax.axis_index("tp") == 1)
        def _():
            attend_heads(range(heads // 2, heads), STEP, 1, *refs)

    return pl.pallas_call(
        kernel,
        out_shape=jax.ShapeDtypeStruct(shape, BF16),
        in_specs=[vmem] * 4 + [hbm],
        out_specs=hbm,
        input_output_aliases={4: 0},
        scratch_shapes=[
            pltpu.VMEM(shape, BF16),
            pltpu.SemaphoreType.DMA((heads * shape[0] // STEP,)),
        ],
        compiler_params=pltpu.CompilerParams(vmem_limit_bytes=VMEM_LIMIT),
        name="attend_late",
    )(document_query, received, document_key, document_value, ctx_out)


def body(
    document_query,
    document_key,
    document_value,
    query_token_query,
    query_token_key,
    query_token_value,
):
    rows, width = document_key.shape
    planes, lines, root_planes = exchange_groups()
    peers = len(planes[0])
    chunk = rows // 2 // peers
    helpers = [plane[1] for plane in root_planes]
    moved = lax.ppermute(document_value, AXES, [tuple(plane[:2]) for plane in root_planes])
    inputs = (
        query_token_query,
        query_token_key,
        query_token_value,
        document_key,
        document_value,
    )
    send = passing_on(local_parts(inputs), moved, helpers)
    received = exchange(send, planes)
    send = middle(received, chunk, len(lines[0]), False)
    received = exchange(send, lines)
    send = middle(received, chunk, peers, True)
    received = exchange(send, planes)
    answer_half = answer_rows(received, query_token_query.shape[1])
    inputs = (document_query, received, document_key, document_value)
    ctx_out, sent_half = attend_early(*inputs, answer_half)
    other_half = lax.ppermute(sent_half, "tp", [(0, 1), (1, 0)])
    ctx_out = attend_late(*inputs, ctx_out)
    first = lax.axis_index("tp") == 0
    halves = (
        jnp.where(first, answer_half, other_half),
        jnp.where(first, other_half, answer_half),
    )
    return (ctx_out, jnp.concatenate(halves, axis=1))


def solution(mesh):
    grid = Mesh(mesh.devices.reshape(SIZES + (-1,)), ("y", "x", "z", "tp"))
    blk = ("y", "x", "z")
    placed = (P(blk, "tp"),) * 3 + (P(None, "tp"),) * 3
    return jax.shard_map(
        body, mesh=grid, in_specs=placed, out_specs=(P(blk, "tp"), P()), check_vma=False
    )
```
